128 devices in a mesh: coef: 8 (over x, y_hi), obs: 16 (over z, y_lo, core).
Axes of the slice: x: 4, y: 4 (y_hi: 2, y_lo: 2; y = y_hi * 2 + y_lo), z: 4, core: 2. Of those that a mesh axis runs over, the one named last changes fastest.
Arguments:
- sample_index: int32 [16384], P('obs'), may hold values from 0 to 16383
- colatitude: float32 [16384], replicated, may hold values from 0.12 to 3.02
- longitude: float32 [16384], replicated, may hold values from -3.140625 to 3.140625
- orders: int32 [128], P('coef'), may hold values from 1 to 237
- observed: float32 [16384], P('obs'), may hold values from -6 to 6
- whitening: bfloat16 [16384, 1024], P('obs')
Outputs:
- normal: float32 [8192, 8192], P(('coef', 'obs'))
- rhs: float32 [8192], P('coef')
The draws below stay inside these ranges and needn't reach their ends.
Inputs may be any that keep to these rules, and one draw needn't show every extreme that they name: `orders`: so every degree m + l stays at most 300.
All inputs are finite; a program needn't handle non-finite values.
Results may differ from the reference program's by a relative error of at most 0.019.
Values may be sent and summed in bfloat16 or wider, within the bound.
A program may use at most 128 MiB of HBM per device.

```python
import jax
import jax.numpy as jnp
from jax import lax

K = 8192
LEV = 64
NMAX = 300
SAMPLES = 16384
R_DEV = 1024
SLOTS = 128
ROWS = 16384
N_OBS = 16


def draw_whitening(key, part):
    key = jax.random.fold_in(key, 7)
    first_key, second_key = jax.random.split(key)
    row_pos = (jnp.arange(ROWS) % R_DEV)[:, None]
    col_pos = jnp.arange(R_DEV)[None, :]
    diagonal = jax.random.uniform(first_key, (ROWS, 1), jnp.float32, 1.0, 2.0)
    below = jax.random.normal(second_key, (ROWS, R_DEV), jnp.float32) * (0.6 / jnp.sqrt(jnp.float32(R_DEV)))
    result = jnp.where(col_pos == row_pos, diagonal, jnp.where(col_pos < row_pos, below, 0.0))
    return result.astype(jnp.bfloat16)


def touch_ends(entries, rng, least, high):
    dims = entries.shape
    index_at = [jax.random.randint(jax.random.fold_in(rng, axis), (), 0, dims[axis]) for axis in range(len(dims))]
    entries = entries.at[tuple(index_at)].set(least)
    longest = dims.index(max(dims))
    index_at[longest] = (index_at[longest] + 1) % dims[longest]
    return entries.at[tuple(index_at)].set(high)


def steps_of(key, shape, pieces, low, high):
    loudness, own = 1.0, jax.random.fold_in(key, 6)
    for axis_at, parts in pieces:
        steps = jnp.exp(jax.random.uniform(jax.random.fold_in(own, axis_at), (parts,), jnp.float32, low / len(pieces), high / len(pieces)))
        loudness = loudness * jnp.repeat(steps, shape[axis_at] // parts).reshape([-1 if axis == axis_at else 1 for axis in range(len(shape))])
    return loudness


def centred(stream_key, dims, deviation, bound, pieces=(), kind=jnp.bfloat16):
    entries = deviation * jax.random.normal(stream_key, dims, jnp.float32)
    if pieces:
        entries = entries * steps_of(stream_key, dims, pieces, -0.22, 0.18)
    return jnp.clip(entries, -bound, bound).astype(kind)


def setup_inputs(seed: int = 0) -> dict:
    splits = jax.random.split(jax.random.key(seed), 7)
    sample_index = touch_ends(jax.random.randint(splits[0], (ROWS,), 0, SAMPLES), jax.random.fold_in(splits[0], 1), 0, SAMPLES - 1).astype(jnp.int32)
    colatitude = jnp.clip(jax.random.uniform(splits[1], (SAMPLES,), jnp.float32, 0.12, 3.02), 0.12, 3.02)
    longitude = jnp.clip(jax.random.uniform(splits[2], (SAMPLES,), jnp.float32, -3.140625, 3.140625), -3.140625, 3.140625)
    orders = touch_ends(jax.random.randint(splits[3], (SLOTS,), 1, NMAX - LEV + 2), jax.random.fold_in(splits[3], 1), 1, (NMAX - LEV + 2) - 1).astype(jnp.int32)
    observed = centred(splits[4], (ROWS,), 1.0, 6.0, ((0, 16),), jnp.float32)
    whitening = draw_whitening(jax.random.fold_in(splits[6], 71), 0)
    return {"sample_index": sample_index, "colatitude": colatitude, "longitude": longitude, "orders": orders, "observed": observed, "whitening": whitening}


def legendre_block(colat_rows, long_rows, orders, parity):
    order_val = orders.astype(jnp.float32)[:, None]
    counter = jnp.arange(1, NMAX + 1, dtype=jnp.float32)[None, :]
    log_const = lax.optimization_barrier(jnp.sum(jnp.where(counter <= order_val, 0.5 * jnp.log((2.0 * counter + 1.0) / (2.0 * counter)), 0.0), axis=1, keepdims=True))
    sectorial = jnp.sqrt(jnp.float32(2.0)) * jnp.exp(log_const + order_val * jnp.log(jnp.sin(colat_rows))[None, :])
    cosine = jnp.cos(colat_rows)[None, :]

    def level(carry, degree_step):
        lower, lowest = carry
        degree = order_val + degree_step
        rise_term = jnp.sqrt((2.0 * degree - 1.0) * (2.0 * degree + 1.0) / ((degree - order_val) * (degree + order_val)))
        fall_term = jnp.sqrt((2.0 * degree + 1.0) * (degree + order_val - 1.0) * (degree - order_val - 1.0) / ((2.0 * degree - 3.0) * (degree + order_val) * (degree - order_val)))
        value = rise_term * cosine * lower - fall_term * lowest
        return ((value, lower), value)
    _, higher = lax.scan(level, (sectorial, jnp.zeros_like(sectorial)), jnp.arange(1, LEV, dtype=jnp.float32))
    levels = jnp.concatenate([sectorial[None], higher], axis=0)
    phase_arg = order_val * long_rows[None, :]
    harmonic = jnp.where(parity[:, None] == 0, jnp.cos(phase_arg), jnp.sin(phase_arg))
    result = jnp.transpose(levels, (1, 0, 2)) * harmonic[:, None, :]
    return result.reshape(orders.shape[0] * LEV, colat_rows.shape[0])

def reference(sample_index, colatitude, longitude, orders, observed, whitening):
    parity = jnp.arange(SLOTS, dtype=jnp.int32) % 2
    inv_rows = 1.0 / ROWS

    def segment(carry, seg_pos):
        normal_acc, rhs_acc = carry
        begin = (seg_pos * R_DEV).astype(jnp.int32)
        index_rows = lax.dynamic_slice_in_dim(sample_index, begin, R_DEV, 0)
        filt_rows = lax.dynamic_slice_in_dim(whitening, begin, R_DEV, 0)
        obs_rows = lax.dynamic_slice_in_dim(observed, begin, R_DEV, 0)
        design = legendre_block(colatitude[index_rows], longitude[index_rows], orders, parity).astype(jnp.bfloat16)
        filtered = lax.dot_general(design, filt_rows, (((1,), (1,)), ((), ())), preferred_element_type=jnp.float32).astype(jnp.bfloat16)
        whitened = jnp.dot(filt_rows.astype(jnp.float32), obs_rows, precision=lax.Precision.HIGHEST)
        gram_part = jnp.dot(filtered, filtered.T, preferred_element_type=jnp.float32) * inv_rows
        gram_part = lax.optimization_barrier(gram_part.astype(jnp.bfloat16)).astype(jnp.float32)
        rhs_part = jnp.dot(filtered.astype(jnp.float32), whitened, precision=lax.Precision.HIGHEST)
        return ((normal_acc + gram_part, rhs_acc + rhs_part), None)
    start = (jnp.zeros((K, K), jnp.float32), jnp.zeros((K,), jnp.float32))
    (normal, rhs_total), _ = lax.scan(segment, start, jnp.arange(N_OBS, dtype=jnp.int32))
    return (normal, rhs_total / jnp.sqrt(jnp.float32(ROWS)))
```

```python
import functools
import math

import jax
import jax.numpy as jnp
from jax import lax
from jax.experimental import pallas as pl
from jax.experimental.pallas import tpu as pltpu
from jax.sharding import PartitionSpec as P

LEV = 64
NMAX = 300
SEG = 1024
SET = 512
NSETS = 16
NEAR = 9
MIRROR = 7
TILE = 256
PITCH = 65
F32 = jnp.float32
BF16 = jnp.bfloat16
MESH = pl.DeviceIdType.MESH
NT = (((1,), (1,)), ((), ()))
COS_TERMS = [(-1.0) ** i * (2.0 * math.pi) ** (2 * i) / math.factorial(2 * i) for i in range(11)]


def prep_kernel(index_ref, colat_ref, long_ref, orders_ref, observed_ref, rows_ref, table_ref):
    index = index_ref[...]
    high, low = index // 128, index % 128
    pos = lax.broadcasted_iota(jnp.int32, (128, SEG), 0)
    pick_high = (pos == high).astype(F32)
    pick_low = (pos == low).astype(F32)

    def look_up(table):
        found = lax.dot_general(
            table, pick_high, (((0,), (0,)), ((), ())),
            precision=lax.Precision.HIGHEST, preferred_element_type=F32,
        )
        return jnp.sum(found * pick_low, axis=0, keepdims=True)

    colat = look_up(colat_ref[...])
    longitude = look_up(long_ref[...])
    rows_ref[...] = jnp.zeros(rows_ref.shape, F32)
    rows_ref[0:1, :] = jnp.log(jnp.sin(colat))
    rows_ref[1:2, :] = jnp.cos(colat)
    rows_ref[2:3, :] = longitude * (0.5 / math.pi)
    rows_ref[3:4, :] = observed_ref[...]

    order = orders_ref[...].astype(F32)
    counter = (lax.broadcasted_iota(jnp.int32, (16, 384), 1) + 1).astype(F32)
    log_const = jnp.sum(
        jnp.where(counter <= order, 0.5 * jnp.log((2.0 * counter + 1.0) / (2.0 * counter)), 0.0),
        axis=1, keepdims=True,
    )
    lane = lax.broadcasted_iota(jnp.int32, (16, 128), 1)
    step = jnp.maximum(lane % 64, 1).astype(F32)
    degree = order + step
    rise = jnp.sqrt((2.0 * degree - 1.0) * (2.0 * degree + 1.0) / (step * (degree + order)))
    fall = jnp.sqrt(
        (2.0 * degree + 1.0) * (degree + order - 1.0) * (step - 1.0)
        / ((2.0 * degree - 3.0) * (degree + order) * step)
    )
    table = jnp.where(lane < 64, rise, fall)
    table = jnp.where(lane == 0, order, table)
    table_ref[...] = jnp.where(lane == 64, log_const, table)


def split_rows(row):
    high = row.astype(BF16).astype(F32)
    rest = row - high
    middle = rest.astype(BF16).astype(F32)
    low = rest - middle
    place = lax.broadcasted_iota(jnp.int32, (16, row.shape[1]), 0)
    pieces = jnp.where(place == 0, high, jnp.where(place == 1, middle, jnp.where(place == 2, low, 0.0)))
    return pieces.astype(BF16)


def main_kernel(
    rows_ref, table_ref, white_ref, out_ref, rhs_ref,
    tab, rows_o, white_o, dscr, dbf, filt, left, wv, own,
    sK, rK, sZ, rZ, sY, rY, keepA, keepB, tot, sT, rT, sR, rR,
    table_s, table_r, rows_s, rows_r, white_s, white_r,
    k_s, k_r, z_s, z_r, y_s, y_r, t_s, t_r, r_s, r_r,
):
    c, o = lax.axis_index("coef"), lax.axis_index("obs")
    x, y_hi = c // 2, c % 2
    z, y_lo, k = o // 4, (o // 2) % 2, o % 2
    y = 2 * y_hi + y_lo
    here = 2 * c + y_lo

    def at(xx, yy, zz, kk):
        return {"coef": 2 * xx + yy // 2, "obs": 4 * zz + 2 * (yy % 2) + kk}

    z_odd = z + 1 - 2 * (z % 2)
    sibling = at(x, y, z, 1 - k)
    z_first = at(x, y, z_odd, k)
    z_second = at(x, y, 3 - z, k)
    y_up = at(x, (y + 1) % 4, z, k)
    y_down = at(x, (y + 3) % 4, z, k)
    y_pair = at(x, y + 1 - 2 * y_lo, z, k)
    near = [sibling, z_first, z_second, y_up, y_down]
    near += [{"coef": (c + j) % 8, "obs": o} for j in range(1, 8)]

    def copy(src, dst, send, recv, device):
        return pltpu.make_async_remote_copy(
            src_ref=src, dst_ref=dst, send_sem=send, recv_sem=recv,
            device_id=device, device_id_type=MESH,
        )

    barrier = pltpu.get_barrier_semaphore()
    for device in near:
        pl.semaphore_signal(barrier, inc=1, device_id=device, device_id_type=MESH)
    pl.semaphore_wait(barrier, len(near))

    tables = [
        copy(table_ref, tab.at[pl.ds(2 * c, 2)], table_s.at[j - 1], table_r.at[j - 1],
             {"coef": (c + j) % 8, "obs": o})
        for j in range(1, 8)
    ]
    for t in tables:
        t.start()
    row_copy = copy(rows_ref, rows_o, rows_s, rows_r, y_up)
    row_copy.start()
    parts = [(3, 0), (0, 0), (2, 1), (1, 1)]
    whites = []
    for n, (block, way) in enumerate(parts):
        area = (pl.ds(block * TILE, TILE), pl.ds(0, (block + 1) * TILE))
        whites.append(copy(white_ref.at[area], white_o.at[area], white_s.at[n], white_r.at[n],
                           y_up if way == 0 else y_down))
    for w in whites:
        w.start()
    tab[pl.ds(2 * c, 2)] = table_ref[...]

    parity = (lax.broadcasted_iota(jnp.int32, (8, SEG), 0) % 2).astype(F32)

    def triangular(operand, white, put):
        for block in range(SEG // TILE):
            depth = (block + 1) * TILE
            put(block, lax.dot_general(
                operand[:, :depth], white[pl.ds(block * TILE, TILE), pl.ds(0, depth)], NT,
                preferred_element_type=F32))

    def keep_level(level, value):
        for part in range(8):
            dscr[part, pl.ds(level, 8, stride=PITCH), :] = value[:, part * 128:(part + 1) * 128]

    def make_filtered(rows, white, d, column):
        coefs = tab[(here + d) % NSETS]
        order, log_const = coefs[:, 0:1], coefs[:, 64:65]
        sectorial = math.sqrt(2.0) * jnp.exp(log_const + order * rows[0:1, :])
        cosine = jnp.broadcast_to(rows[1:2, :], (8, SEG))
        turn = order * rows[2:3, :] - 0.25 * parity
        turn = turn - jnp.floor(turn + 0.5)
        square = turn * turn
        harmonic = jnp.full_like(square, COS_TERMS[-1])
        for term in COS_TERMS[-2::-1]:
            harmonic = harmonic * square + term
        lower = sectorial * harmonic
        lowest = jnp.zeros_like(lower)
        keep_level(0, lower)
        for level in range(1, LEV):
            value = (coefs[:, level:level + 1] * cosine) * lower - coefs[:, 64 + level:65 + level] * lowest
            keep_level(level, value)
            lower, lowest = value, lower
        for slot in range(8):
            for part in range(8):
                dbf[slot * LEV:(slot + 1) * LEV, part * 128:(part + 1) * 128] = (
                    dscr[part, slot * PITCH:slot * PITCH + LEV, :].astype(BF16))

        def put(block, value):
            filt[d, :, pl.ds(column + block * TILE, TILE)] = value.astype(BF16)

        triangular(dbf, white, put)

    def make_whitened(rows, white, column):
        pieces = split_rows(rows[3:4, :])

        def put(block, value):
            row = jnp.sum(value, axis=0, keepdims=True)
            wv[:, pl.ds(column + block * TILE, TILE)] = split_rows(row)

        triangular(pieces, white, put)

    make_filtered(rows_ref, white_ref, 0, 0)
    make_whitened(rows_ref, white_ref, 0)
    for t in tables:
        t.wait()

    def first(d, carry):
        make_filtered(rows_ref, white_ref, d, 0)
        return carry

    lax.fori_loop(1, NEAR, first, 0)
    row_copy.wait()
    for w in whites:
        w.wait()
    make_filtered(rows_o, white_o, 0, SEG)
    make_whitened(rows_o, white_o, SEG)
    order_z = [z, 3 - z, 3 - z_odd, z_odd]
    for half, kk in enumerate((1 - k, k)):
        for n, zz in enumerate(order_z):
            left[pl.ds(half * 256 + n * 64, 64), :] = filt[0, pl.ds(pl.multiple_of((2 * zz + kk) * 64, 64), 64), :]

    rhs_part = lax.dot_general(wv[...], filt[0], NT, preferred_element_type=F32)
    rhs_sum = jnp.sum(rhs_part, axis=0, keepdims=True)
    sR[0] = jnp.broadcast_to(rhs_sum, (8, SET))

    def rhs_copy(n):
        return copy(sR.at[n], rR.at[n], r_s.at[n], r_r.at[n], (sibling, z_first, z_second, y_pair)[n])

    rhs_copy(0).start()

    def rhs_step(n):
        rhs_copy(n).wait()
        if n < 3:
            sR[n + 1] = sR[n] + rR[n]
            rhs_copy(n + 1).start()
        else:
            scale = 1.0 / math.sqrt(16.0 * SEG)
            for zz in range(4):
                lanes = slice(zz * 128, (zz + 1) * 128)
                rhs_ref[0:1, pl.ds(pl.multiple_of(zz * 256 + y_lo * 128, 128), 128)] = scale * sR[3, 0:1, lanes]
                rhs_ref[0:1, pl.ds(pl.multiple_of(zz * 256 + (1 - y_lo) * 128, 128), 128)] = scale * rR[3, 0:1, lanes]

    inv_rows = 1.0 / (16.0 * SEG)

    def set_of(j):
        return (j + 1) % NEAR

    def base_of(q):
        return (q // 2) * 1024 + (q % 2) * 128

    def k_copy(j):
        return copy(sK.at[j], rK.at[j], k_s.at[j], k_r.at[j], sibling)

    def z_copies(j):
        return [copy(sZ.at[j, h], rZ.at[j, h], z_s.at[j, h], z_r.at[j, h], (z_first, z_second)[h]) for h in range(2)]

    def y_copies(j):
        return [copy(sY.at[j, h], rY.at[j, h], y_s.at[j, h], y_r.at[j, h], (z_second, z_first)[h]) for h in range(2)]

    def t_copy(j, slot):
        q = (here + j + 1) % NSETS
        return copy(sT.at[j, slot], rT.at[j, 2 * z + k], t_s.at[j, slot], t_r.at[j],
                    at(q // 4, q % 4, slot // 2, slot % 2))

    def finish(j):
        for move in y_copies(j):
            move.wait_recv()
        total = tot[...] + jnp.concatenate([rY[j, 0], rY[j, 1]], axis=1).astype(F32)
        base = base_of((here + set_of(j)) % NSETS)
        for zz in range(4):
            out_ref[:, pl.ds(pl.multiple_of(base + zz * 256, 128), 128)] = inv_rows * total[:, zz * 128:(zz + 1) * 128]

        @pl.when(j < MIRROR)
        def _():
            turned = total.T
            for slot in range(8):
                sT[j, slot] = jnp.concatenate(
                    [turned[slot * 64:slot * 64 + 32], turned[slot * 64 + 32:slot * 64 + 64]], axis=1).astype(BF16)

            def send(slot, carry):
                t_copy(j, slot).start()
                return carry

            lax.fori_loop(0, 8, send, 0)

    def second(j):
        for move in z_copies(j):
            move.wait_recv()
        sY[j, 0] = (keepA[64:128, :] + rZ[j, 0, 0:64, :].astype(F32)).astype(BF16)
        sY[j, 1] = (keepB[64:128, :] + rZ[j, 1, 64:128, :].astype(F32)).astype(BF16)
        for move in y_copies(j):
            move.start()
        tot[:, 0:256] = keepA[0:64, :] + rZ[j, 0, 64:128, :].astype(F32)
        tot[:, 256:512] = keepB[0:64, :] + rZ[j, 1, 0:64, :].astype(F32)

    def third(j):
        k_copy(j).wait_recv()
        sZ[j, 0] = (own[128:256, 0:256] + rK[j, 128:256, 0:256].astype(F32)).astype(BF16)
        sZ[j, 1] = (own[64:192, 256:512] + rK[j, 64:192, 256:512].astype(F32)).astype(BF16)
        for move in z_copies(j):
            move.start()
        keepA[...] = own[0:128, 0:256] + rK[j, 0:128, 0:256].astype(F32)
        keepB[0:64, :] = own[0:64, 256:512] + rK[j, 0:64, 256:512].astype(F32)
        keepB[64:128, :] = own[192:256, 256:512] + rK[j, 192:256, 256:512].astype(F32)

    def gram(j):
        d = set_of(j)
        for n in range(2):
            part = lax.dot_general(left[...], filt[d, n * 256:(n + 1) * 256, :], NT, preferred_element_type=F32)
            sK[j, :, n * 256:(n + 1) * 256] = part[0:256].astype(BF16)
            own[:, n * 256:(n + 1) * 256] = part[256:512]
        k_copy(j).start()

    def stage(i, carry):
        @pl.when(i < NEAR - 1)
        def _():
            make_filtered(rows_o, white_o, i + 1, SEG)

        for n in range(4):
            @pl.when(i == n)
            def _(n=n):
                rhs_step(n)

        @pl.when(i >= 3)
        def _():
            finish(i - 3)

        @pl.when((i >= 2) & (i < NEAR + 2))
        def _():
            second(i - 2)

        @pl.when((i >= 1) & (i < NEAR + 1))
        def _():
            third(i - 1)

        @pl.when(i < NEAR)
        def _():
            gram(i)

        return carry

    lax.fori_loop(0, NEAR + 3, stage, 0)

    def mirrored(j, carry):
        copy(sT.at[j], rT.at[j], t_s.at[j, 0], t_r.at[j], sibling).wait_recv()
        base = base_of((here + NSETS - 1 - j) % NSETS)
        for zz in range(4):
            for half in range(2):
                lanes = slice(half * 64, half * 64 + 64)
                piece = jnp.concatenate(
                    [rT[j, 2 * zz, :, lanes].astype(F32), rT[j, 2 * zz + 1, :, lanes].astype(F32)], axis=1)
                out_ref[half * 32:half * 32 + 32, pl.ds(pl.multiple_of(base + zz * 256, 128), 128)] = inv_rows * piece

        def sent(slot, inner):
            t_copy(j, slot).wait_send()
            return inner

        lax.fori_loop(0, 8, sent, 0)
        return carry

    lax.fori_loop(0, MIRROR, mirrored, 0)

    def drain(j, carry):
        k_copy(j).wait_send()
        for move in z_copies(j) + y_copies(j):
            move.wait_send()
        return carry

    lax.fori_loop(0, NEAR, drain, 0)


def on_device(sample_index, colatitude, longitude, orders, observed, whitening):
    vmem = pl.BlockSpec(memory_space=pltpu.VMEM)
    shaped_orders = orders.reshape(4, 2, 2).transpose(1, 0, 2).reshape(16, 1)
    rows, table = pl.pallas_call(
        prep_kernel,
        out_shape=(jax.ShapeDtypeStruct((8, SEG), F32), jax.ShapeDtypeStruct((16, 128), F32)),
        in_specs=[vmem] * 5,
        out_specs=(vmem, vmem),
    )(
        sample_index.reshape(1, SEG), colatitude.reshape(128, 128), longitude.reshape(128, 128),
        shaped_orders, observed.reshape(1, SEG),
    )
    V = pltpu.VMEM
    dma = pltpu.SemaphoreType.DMA
    normal, rhs = pl.pallas_call(
        main_kernel,
        out_shape=(jax.ShapeDtypeStruct((64, 8192), F32), jax.ShapeDtypeStruct((1, SEG), F32)),
        in_specs=[vmem] * 3,
        out_specs=(vmem, vmem),
        scratch_shapes=[
            V((NSETS, 8, 128), F32), V((8, SEG), F32), V((SEG, SEG), BF16),
            V((8, 8 * PITCH, 128), F32), V((SET, SEG), BF16), V((NEAR, SET, 2 * SEG), BF16),
            V((SET, 2 * SEG), BF16), V((16, 2 * SEG), BF16), V((256, SET), F32),
            V((NEAR, 256, SET), BF16), V((NEAR, 256, SET), BF16),
            V((NEAR, 2, 128, 256), BF16), V((NEAR, 2, 128, 256), BF16),
            V((NEAR, 2, 64, 256), BF16), V((NEAR, 2, 64, 256), BF16),
            V((128, 256), F32), V((128, 256), F32), V((64, SET), F32),
            V((MIRROR, 8, 32, 128), BF16), V((MIRROR, 8, 32, 128), BF16),
            V((4, 8, SET), F32), V((4, 8, SET), F32),
            dma((7,)), dma((7,)), dma, dma, dma((4,)), dma((4,)),
            dma((NEAR,)), dma((NEAR,)), dma((NEAR, 2)), dma((NEAR, 2)),
            dma((NEAR, 2)), dma((NEAR, 2)), dma((MIRROR, 8)), dma((MIRROR,)),
            dma((4,)), dma((4,)),
        ],
        compiler_params=pltpu.CompilerParams(
            collective_id=0, has_side_effects=True, vmem_limit_bytes=58 * 2**20,
        ),
    )(rows, table.reshape(2, 8, 128), whitening)
    return normal, rhs.reshape(SEG)


def solution(mesh):
    placed = (P("obs"), P(), P(), P("coef"), P("obs"), P("obs", None))
    return jax.shard_map(
        on_device,
        mesh=mesh,
        in_specs=placed,
        out_specs=(P(("coef", "obs"), None), P("coef")),
        check_vma=False,
    )
```

```python
import functools
import math

import jax
import jax.numpy as jnp
from jax import lax
from jax.experimental import pallas as pl
from jax.experimental.pallas import tpu as pltpu
from jax.sharding import PartitionSpec as P

LEV = 64
NMAX = 300
SEG = 1024
SET = 512
NSETS = 16
NEAR = 9
MIRROR = 7
TILE = 256
PITCH = 65
F32 = jnp.float32
BF16 = jnp.bfloat16
MESH = pl.DeviceIdType.MESH
NT = (((1,), (1,)), ((), ()))
COS_TERMS = [(-1.0) ** i * (2.0 * math.pi) ** (2 * i) / math.factorial(2 * i) for i in range(11)]


def prepare(index_ref, colat_ref, long_ref, orders_ref, observed_ref, rows_ref):
    index = index_ref[...]
    high, low = index // 128, index % 128
    pos = lax.broadcasted_iota(jnp.int32, (128, SEG), 0)
    pick_high = (pos == high).astype(F32)
    pick_low = (pos == low).astype(F32)

    def look_up(table):
        found = lax.dot_general(
            table, pick_high, (((0,), (0,)), ((), ())),
            precision=lax.Precision.HIGHEST, preferred_element_type=F32,
        )
        return jnp.sum(found * pick_low, axis=0, keepdims=True)

    colat = look_up(colat_ref[...])
    longitude = look_up(long_ref[...])
    rows_ref[...] = jnp.zeros(rows_ref.shape, F32)
    rows_ref[0:1, :] = jnp.log(jnp.sin(colat))
    rows_ref[1:2, :] = jnp.cos(colat)
    rows_ref[2:3, :] = longitude * (0.5 / math.pi)
    rows_ref[3:4, :] = observed_ref[...]

    place = lax.broadcasted_iota(jnp.int32, (16, 16), 0)
    wanted = (place // 2 % 4) * 4 + (place // 8) * 2 + place % 2
    given = lax.broadcasted_iota(jnp.int32, (16, 16), 1)
    order = jnp.sum(jnp.where(given == wanted, orders_ref[...].astype(F32), 0.0), axis=1, keepdims=True)
    counter = (lax.broadcasted_iota(jnp.int32, (16, 384), 1) + 1).astype(F32)
    log_const = jnp.sum(
        jnp.where(counter <= order, 0.5 * jnp.log((2.0 * counter + 1.0) / (2.0 * counter)), 0.0),
        axis=1, keepdims=True,
    )
    lane = lax.broadcasted_iota(jnp.int32, (16, 128), 1)
    step = jnp.maximum(lane % 64, 1).astype(F32)
    degree = order + step
    rise = jnp.sqrt((2.0 * degree - 1.0) * (2.0 * degree + 1.0) / (step * (degree + order)))
    fall = jnp.sqrt(
        (2.0 * degree + 1.0) * (degree + order - 1.0) * (step - 1.0)
        / ((2.0 * degree - 3.0) * (degree + order) * step)
    )
    table = jnp.where(lane < 64, rise, fall)
    table = jnp.where(lane == 0, order, table)
    return jnp.where(lane == 64, log_const, table)


def interleave(*parts):
    parts = list(parts)
    while parts:
        for part in list(parts):
            try:
                next(part)
            except StopIteration:
                parts.remove(part)


def split_rows(row):
    high = row.astype(BF16).astype(F32)
    rest = row - high
    middle = rest.astype(BF16).astype(F32)
    low = rest - middle
    place = lax.broadcasted_iota(jnp.int32, (16, row.shape[1]), 0)
    pieces = jnp.where(place == 0, high, jnp.where(place == 1, middle, jnp.where(place == 2, low, 0.0)))
    return pieces.astype(BF16)


def main_kernel(
    index_ref, colat_ref, long_ref, orders_ref, observed_ref, white_ref, out_ref, rhs_ref,
    tab, rows_l, rows_o, white_l, white_o, dscr, dbfA, dbfB, filt, left, wv, own,
    sK, rK, sZ, rZ, sY, rY, keepA, keepB, tot, sT, rT, sR, rR,
    load_s, table_s, table_r, rows_s, rows_r, white_s, white_r,
    k_s, k_r, z_s, z_r, y_s, y_r, t_s, t_r, r_s, r_r,
):
    c, o = lax.axis_index("coef"), lax.axis_index("obs")
    x, y_hi = c // 2, c % 2
    z, y_lo, k = o // 4, (o // 2) % 2, o % 2
    y = 2 * y_hi + y_lo
    here = 2 * c + y_lo

    def at(xx, yy, zz, kk):
        return {"coef": 2 * xx + yy // 2, "obs": 4 * zz + 2 * (yy % 2) + kk}

    z_odd = z + 1 - 2 * (z % 2)
    sibling = at(x, y, z, 1 - k)
    z_first = at(x, y, z_odd, k)
    z_second = at(x, y, 3 - z, k)
    y_up = at(x, (y + 1) % 4, z, k)
    y_down = at(x, (y + 3) % 4, z, k)
    y_pair = at(x, y + 1 - 2 * y_lo, z, k)
    near = [sibling, z_first, z_second, y_up, y_down]
    near += [{"coef": (c + j) % 8, "obs": o} for j in range(1, 8)]

    def copy(src, dst, send, recv, device):
        return pltpu.make_async_remote_copy(
            src_ref=src, dst_ref=dst, send_sem=send, recv_sem=recv,
            device_id=device, device_id_type=MESH,
        )

    barrier = pltpu.get_barrier_semaphore()
    for device in near:
        pl.semaphore_signal(barrier, inc=1, device_id=device, device_id_type=MESH)
    load = pltpu.make_async_copy(white_ref, white_l, load_s)
    load.start()
    table = prepare(index_ref, colat_ref, long_ref, orders_ref, observed_ref, rows_l)
    tab[2 * c] = table[0:8]
    tab[2 * c + 1] = table[8:16]
    pl.semaphore_wait(barrier, len(near))

    def table_copy(j):
        mine = tab.at[pl.ds(2 * c, 2)]
        return copy(mine, mine, table_s.at[j - 1], table_r.at[j - 1], {"coef": (c + 8 - j) % 8, "obs": o})

    for j in range(1, 5):
        table_copy(j).start()
    row_copy = copy(rows_l, rows_o, rows_s, rows_r, y_up)
    row_copy.start()
    whites = []
    for n, (block, way) in enumerate([(3, 0), (2, 1), (0, 0), (1, 1)]):
        area = (pl.ds(block * TILE, TILE), pl.ds(0, (block + 1) * TILE))
        whites.append(copy(white_ref.at[area], white_o.at[area], white_s.at[n], white_r.at[n],
                           y_up if way == 0 else y_down))
    for w in whites:
        w.start()

    parity = (lax.broadcasted_iota(jnp.int32, (8, SEG), 0) % 2).astype(F32)

    def triangular(operand, white, put):
        for block in range(SEG // TILE):
            depth = (block + 1) * TILE
            put(block, lax.dot_general(
                operand[:, :depth], white[pl.ds(block * TILE, TILE), pl.ds(0, depth)], NT,
                preferred_element_type=F32))

    def keep_level(level, value):
        for part in range(8):
            dscr[part, pl.ds(level, 8, stride=PITCH), :] = value[:, part * 128:(part + 1) * 128]

    def design(rows, d, dbf):
        coefs = tab[(here + d) % NSETS]
        order, log_const = coefs[:, 0:1], coefs[:, 64:65]
        sectorial = math.sqrt(2.0) * jnp.exp(log_const + order * rows[0:1, :])
        cosine = jnp.broadcast_to(rows[1:2, :], (8, SEG))
        turn = order * rows[2:3, :] - 0.25 * parity
        turn = turn - jnp.floor(turn + 0.5)
        square = turn * turn
        harmonic = jnp.full_like(square, COS_TERMS[-1])
        for term in COS_TERMS[-2::-1]:
            harmonic = harmonic * square + term
        lower = sectorial * harmonic
        lowest = jnp.zeros_like(lower)
        keep_level(0, lower)
        for level in range(1, LEV):
            value = (coefs[:, level:level + 1] * cosine) * lower - coefs[:, 64 + level:65 + level] * lowest
            keep_level(level, value)
            lower, lowest = value, lower
            if level % 8 == 7:
                yield
        for slot in range(8):
            for part in range(8):
                dbf[slot * LEV:(slot + 1) * LEV, part * 128:(part + 1) * 128] = (
                    dscr[part, slot * PITCH:slot * PITCH + LEV, :].astype(BF16))
            yield

    def whiten(white, d, dbf, column):
        for block in range(SEG // TILE):
            depth = (block + 1) * TILE
            value = lax.dot_general(
                dbf[:, :depth], white[block * TILE:(block + 1) * TILE, :depth], NT, preferred_element_type=F32)
            filt[d, :, pl.ds(column + block * TILE, TILE)] = value.astype(BF16)
            yield

    def make_whitened(rows, white, column):
        pieces = split_rows(rows[3:4, :])

        def put(block, value):
            row = jnp.sum(value, axis=0, keepdims=True)
            wv[:, pl.ds(column + block * TILE, TILE)] = split_rows(row)

        triangular(pieces, white, put)

    interleave(design(rows_l, 0, dbfA))
    load.wait()
    make_whitened(rows_l, white_l, 0)

    def first(t, carry):
        for j in range(4):
            @pl.when(t == j)
            def _(j=j):
                table_copy(j + 1).wait()

        interleave(whiten(white_l, 2 * t, dbfA, 0), design(rows_l, 2 * t + 1, dbfB))
        interleave(whiten(white_l, 2 * t + 1, dbfB, 0), design(rows_l, 2 * t + 2, dbfA))
        return carry

    lax.fori_loop(0, 4, first, 0)
    row_copy.wait()
    interleave(whiten(white_l, 8, dbfA, 0), design(rows_o, 0, dbfB))
    for w in whites:
        w.wait()
    interleave(whiten(white_o, 0, dbfB, SEG), design(rows_o, 1, dbfA))
    make_whitened(rows_o, white_o, SEG)
    order_z = [z, 3 - z, 3 - z_odd, z_odd]
    for half, kk in enumerate((1 - k, k)):
        for n, zz in enumerate(order_z):
            left[pl.ds(half * 256 + n * 64, 64), :] = filt[0, pl.ds(pl.multiple_of((2 * zz + kk) * 64, 64), 64), :]

    rhs_part = lax.dot_general(wv[...], filt[0], NT, preferred_element_type=F32)
    rhs_sum = jnp.sum(rhs_part, axis=0, keepdims=True)
    sR[0] = jnp.broadcast_to(rhs_sum, (8, SET))

    def rhs_copy(n):
        return copy(sR.at[n], rR.at[n], r_s.at[n], r_r.at[n], (sibling, z_first, z_second, y_pair)[n])

    rhs_copy(0).start()

    def rhs_step(n):
        rhs_copy(n).wait()
        if n < 3:
            sR[n + 1] = sR[n] + rR[n]
            rhs_copy(n + 1).start()
        else:
            for zz in range(4):
                lanes = slice(zz * 128, (zz + 1) * 128)
                rhs_ref[0:1, pl.ds(pl.multiple_of(zz * 256 + y_lo * 128, 128), 128)] = sR[3, 0:1, lanes]
                rhs_ref[0:1, pl.ds(pl.multiple_of(zz * 256 + (1 - y_lo) * 128, 128), 128)] = rR[3, 0:1, lanes]

    def set_of(j):
        return (j + 1) % NEAR

    def base_of(q):
        return (q // 2) * 1024 + (q % 2) * 128

    def k_copy(j):
        return copy(sK.at[j], rK.at[j], k_s.at[j], k_r.at[j], sibling)

    def z_copies(j):
        return [copy(sZ.at[j, h], rZ.at[j, h], z_s.at[j, h], z_r.at[j, h], (z_first, z_second)[h]) for h in range(2)]

    def y_copies(j):
        return [copy(sY.at[j, h], rY.at[j, h], y_s.at[j, h], y_r.at[j, h], (z_second, z_first)[h]) for h in range(2)]

    def t_copy(j, slot):
        q = (here + j + 1) % NSETS
        return copy(sT.at[j, slot], rT.at[j, 2 * z + k], t_s.at[j, slot], t_r.at[j],
                    at(q // 4, q % 4, slot // 2, slot % 2))

    def finish(j):
        for move in y_copies(j):
            move.wait_recv()
        total = tot[j % 2] + jnp.concatenate([rY[j, 0], rY[j, 1]], axis=1).astype(F32)
        base = base_of((here + set_of(j)) % NSETS)
        for zz in range(4):
            out_ref[:, pl.ds(pl.multiple_of(base + zz * 256, 128), 128)] = total[:, zz * 128:(zz + 1) * 128]

        def mirror():
            turned = total.T
            for slot in range(8):
                sT[j, slot] = jnp.concatenate(
                    [turned[slot * 64:slot * 64 + 32], turned[slot * 64 + 32:slot * 64 + 64]], axis=1).astype(BF16)

            def send(slot, carry):
                t_copy(j, slot).start()
                return carry

            lax.fori_loop(0, 8, send, 0)

        if not isinstance(j, int) or j < MIRROR:
            mirror()

    def second(j):
        par = j % 2
        for move in z_copies(j):
            move.wait_recv()
        sY[j, 0] = (keepA[par, 64:128, :] + rZ[j, 0, 0:64, :].astype(F32)).astype(BF16)
        sY[j, 1] = (keepB[par, 64:128, :] + rZ[j, 1, 64:128, :].astype(F32)).astype(BF16)
        for move in y_copies(j):
            move.start()
        tot[par, :, 0:256] = keepA[par, 0:64, :] + rZ[j, 0, 64:128, :].astype(F32)
        tot[par, :, 256:512] = keepB[par, 0:64, :] + rZ[j, 1, 0:64, :].astype(F32)

    def third(j):
        par = j % 2
        k_copy(j).wait_recv()
        sZ[j, 0] = (own[par, 128:256, 0:256] + rK[j, 128:256, 0:256].astype(F32)).astype(BF16)
        sZ[j, 1] = (own[par, 64:192, 256:512] + rK[j, 64:192, 256:512].astype(F32)).astype(BF16)
        for move in z_copies(j):
            move.start()
        keepA[par] = own[par, 0:128, 0:256] + rK[j, 0:128, 0:256].astype(F32)
        keepB[par, 0:64, :] = own[par, 0:64, 256:512] + rK[j, 0:64, 256:512].astype(F32)
        keepB[par, 64:128, :] = own[par, 192:256, 256:512] + rK[j, 192:256, 256:512].astype(F32)

    def gram(j, d):
        for n in range(2):
            part = lax.dot_general(left[...], filt[d, n * 256:(n + 1) * 256, :], NT, preferred_element_type=F32)
            sK[j, :, n * 256:(n + 1) * 256] = part[0:256].astype(BF16)
            own[j % 2, :, n * 256:(n + 1) * 256] = part[256:512]
            yield

    def stage(i, carry):
        for n in range(4):
            @pl.when(i == n)
            def _(n=n):
                rhs_step(n)

        @pl.when(i >= 2)
        def _():
            third(i - 2)

        interleave(whiten(white_o, i + 1, dbfA, SEG))

        @pl.when(i >= 3)
        def _():
            second(i - 3)

        @pl.when(i >= 4)
        def _():
            finish(i - 4)

        interleave(gram(i, i + 1), design(rows_o, jnp.minimum(i + 2, NEAR - 1), dbfA))
        k_copy(i).start()
        return carry

    lax.fori_loop(0, NEAR - 1, stage, 0)
    third(6)
    interleave(gram(8, 0))
    k_copy(8).start()
    second(5)
    finish(4)
    third(7)
    second(6)
    finish(5)
    third(8)
    second(7)
    finish(6)

    def mirrored(j, carry):
        copy(sT.at[j], rT.at[j], t_s.at[j, 0], t_r.at[j], sibling).wait_recv()
        base = base_of((here + NSETS - 1 - j) % NSETS)
        for zz in range(4):
            for half in range(2):
                lanes = slice(half * 64, half * 64 + 64)
                piece = jnp.concatenate(
                    [rT[j, 2 * zz, :, lanes].astype(F32), rT[j, 2 * zz + 1, :, lanes].astype(F32)], axis=1)
                out_ref[half * 32:half * 32 + 32, pl.ds(pl.multiple_of(base + zz * 256, 128), 128)] = piece

        def sent(slot, inner):
            t_copy(j, slot).wait_send()
            return inner

        lax.fori_loop(0, 8, sent, 0)
        return carry

    lax.fori_loop(0, 3, mirrored, 0)
    second(8)
    finish(7)
    lax.fori_loop(3, 5, mirrored, 0)
    finish(8)
    lax.fori_loop(5, MIRROR, mirrored, 0)

    def drain(j, carry):
        k_copy(j).wait_send()
        for move in z_copies(j) + y_copies(j):
            move.wait_send()
        return carry

    lax.fori_loop(0, NEAR, drain, 0)


def on_device(sample_index, colatitude, longitude, orders, observed, whitening):
    vmem = pl.BlockSpec(memory_space=pltpu.VMEM)
    V = pltpu.VMEM
    dma = pltpu.SemaphoreType.DMA
    normal, rhs = pl.pallas_call(
        main_kernel,
        out_shape=(jax.ShapeDtypeStruct((64, 8192), F32), jax.ShapeDtypeStruct((1, SEG), F32)),
        in_specs=[vmem] * 5 + [pl.BlockSpec(memory_space=pl.ANY)],
        out_specs=(vmem, vmem),
        scratch_shapes=[
            V((NSETS, 8, 128), F32), V((8, SEG), F32), V((8, SEG), F32),
            V((SEG, SEG), BF16), V((SEG, SEG), BF16),
            V((8, 8 * PITCH, 128), F32), V((SET, SEG), BF16), V((SET, SEG), BF16),
            V((NEAR, SET, 2 * SEG), BF16),
            V((SET, 2 * SEG), BF16), V((16, 2 * SEG), BF16), V((2, 256, SET), F32),
            V((NEAR, 256, SET), BF16), V((NEAR, 256, SET), BF16),
            V((NEAR, 2, 128, 256), BF16), V((NEAR, 2, 128, 256), BF16),
            V((NEAR, 2, 64, 256), BF16), V((NEAR, 2, 64, 256), BF16),
            V((2, 128, 256), F32), V((2, 128, 256), F32), V((2, 64, SET), F32),
            V((MIRROR, 8, 32, 128), BF16), V((MIRROR, 8, 32, 128), BF16),
            V((4, 8, SET), F32), V((4, 8, SET), F32),
            dma, dma((4,)), dma((4,)), dma, dma, dma((4,)), dma((4,)),
            dma((NEAR,)), dma((NEAR,)), dma((NEAR, 2)), dma((NEAR, 2)),
            dma((NEAR, 2)), dma((NEAR, 2)), dma((MIRROR, 8)), dma((MIRROR,)),
            dma((4,)), dma((4,)),
        ],
        compiler_params=pltpu.CompilerParams(
            collective_id=0, has_side_effects=True, vmem_limit_bytes=60 * 2**20,
        ),
    )(
        sample_index.reshape(1, SEG), colatitude.reshape(128, 128), longitude.reshape(128, 128),
        orders.reshape(1, 16), observed.reshape(1, SEG), whitening,
    )
    rows = 16.0 * SEG
    return normal * (1.0 / rows), rhs.reshape(SEG) * (1.0 / math.sqrt(rows))


def solution(mesh):
    placed = (P("obs"), P(), P(), P("coef"), P("obs"), P("obs", None))
    return jax.shard_map(
        on_device,
        mesh=mesh,
        in_specs=placed,
        out_specs=(P(("coef", "obs"), None), P("coef")),
        check_vma=False,
    )
```

```python
import functools
import math

import jax
import jax.numpy as jnp
from jax import lax
from jax.experimental import pallas as pl
from jax.experimental.pallas import tpu as pltpu
from jax.sharding import PartitionSpec as P

LEV = 64
NMAX = 300
SEG = 1024
SET = 512
NSETS = 16
NEAR = 9
MIRROR = 7
TILE = 256
PITCH = 65
F32 = jnp.float32
BF16 = jnp.bfloat16
MESH = pl.DeviceIdType.MESH
NT = (((1,), (1,)), ((), ()))
COS_TERMS = [(-1.0) ** i * (2.0 * math.pi) ** (2 * i) / math.factorial(2 * i) for i in range(11)]


def prepare(index_ref, colat_ref, long_ref, orders_ref, observed_ref, rows_ref):
    index = index_ref[...]
    high, low = index // 128, index % 128
    pos = lax.broadcasted_iota(jnp.int32, (128, SEG), 0)
    pick_high = (pos == high).astype(F32)
    pick_low = (pos == low).astype(F32)

    def look_up(table):
        found = lax.dot_general(
            table, pick_high, (((0,), (0,)), ((), ())),
            precision=lax.Precision.HIGHEST, preferred_element_type=F32,
        )
        return jnp.sum(found * pick_low, axis=0, keepdims=True)

    colat = look_up(colat_ref[...])
    longitude = look_up(long_ref[...])
    rows_ref[...] = jnp.zeros(rows_ref.shape, F32)
    rows_ref[0:1, :] = jnp.log(jnp.sin(colat))
    rows_ref[1:2, :] = jnp.cos(colat)
    rows_ref[2:3, :] = longitude * (0.5 / math.pi)
    rows_ref[3:4, :] = observed_ref[...]

    place = lax.broadcasted_iota(jnp.int32, (16, 16), 0)
    wanted = (place // 2 % 4) * 4 + (place // 8) * 2 + place % 2
    given = lax.broadcasted_iota(jnp.int32, (16, 16), 1)
    order = jnp.sum(jnp.where(given == wanted, orders_ref[...].astype(F32), 0.0), axis=1, keepdims=True)
    counter = (lax.broadcasted_iota(jnp.int32, (16, 384), 1) + 1).astype(F32)
    log_const = jnp.sum(
        jnp.where(counter <= order, 0.5 * jnp.log((2.0 * counter + 1.0) / (2.0 * counter)), 0.0),
        axis=1, keepdims=True,
    )
    lane = lax.broadcasted_iota(jnp.int32, (16, 128), 1)
    step = jnp.maximum(lane % 64, 1).astype(F32)
    degree = order + step
    rise = jnp.sqrt((2.0 * degree - 1.0) * (2.0 * degree + 1.0) / (step * (degree + order)))
    fall = jnp.sqrt(
        (2.0 * degree + 1.0) * (degree + order - 1.0) * (step - 1.0)
        / ((2.0 * degree - 3.0) * (degree + order) * step)
    )
    table = jnp.where(lane < 64, rise, fall)
    table = jnp.where(lane == 0, order, table)
    return jnp.where(lane == 64, log_const, table)


def interleave(*parts):
    parts = list(parts)
    while parts:
        for part in list(parts):
            try:
                next(part)
            except StopIteration:
                parts.remove(part)


def split_rows(row):
    high = row.astype(BF16).astype(F32)
    rest = row - high
    middle = rest.astype(BF16).astype(F32)
    low = rest - middle
    place = lax.broadcasted_iota(jnp.int32, (16, row.shape[1]), 0)
    pieces = jnp.where(place == 0, high, jnp.where(place == 1, middle, jnp.where(place == 2, low, 0.0)))
    return pieces.astype(BF16)


def main_kernel(
    index_ref, colat_ref, long_ref, orders_ref, observed_ref, white_ref, out_ref, rhs_ref,
    tab, rows_l, rows_o, white_l, white_o, dscr, dbf, filt, part, left, wv, own,
    sK, rK, sZ, rZ, sY, rY, keepA, keepB, tot, sT, rT, sR, rR,
    load_s, table_s, table_r, rows_s, rows_r, white_s, white_r,
    k_s, k_r, z_s, z_r, y_s, y_r, t_s, t_r, r_s, r_r,
):
    c, o = lax.axis_index("coef"), lax.axis_index("obs")
    x, y_hi = c // 2, c % 2
    z, y_lo, k = o // 4, (o // 2) % 2, o % 2
    y = 2 * y_hi + y_lo
    here = 2 * c + y_lo

    def at(xx, yy, zz, kk):
        return {"coef": 2 * xx + yy // 2, "obs": 4 * zz + 2 * (yy % 2) + kk}

    z_odd = z + 1 - 2 * (z % 2)
    sibling = at(x, y, z, 1 - k)
    z_first = at(x, y, z_odd, k)
    z_second = at(x, y, 3 - z, k)
    y_up = at(x, (y + 1) % 4, z, k)
    y_down = at(x, (y + 3) % 4, z, k)
    y_pair = at(x, y + 1 - 2 * y_lo, z, k)
    near = [sibling, z_first, z_second, y_up, y_down]
    near += [{"coef": (c + j) % 8, "obs": o} for j in range(1, 8)]

    def copy(src, dst, send, recv, device):
        return pltpu.make_async_remote_copy(
            src_ref=src, dst_ref=dst, send_sem=send, recv_sem=recv,
            device_id=device, device_id_type=MESH,
        )

    barrier = pltpu.get_barrier_semaphore()
    for device in near:
        pl.semaphore_signal(barrier, inc=1, device_id=device, device_id_type=MESH)
    load = pltpu.make_async_copy(white_ref, white_l, load_s)
    load.start()
    table = prepare(index_ref, colat_ref, long_ref, orders_ref, observed_ref, rows_l)
    tab[2 * c] = table[0:8]
    tab[2 * c + 1] = table[8:16]
    pl.semaphore_wait(barrier, len(near))

    def table_copy(j):
        mine = tab.at[pl.ds(2 * c, 2)]
        return copy(mine, mine, table_s.at[j - 1], table_r.at[j - 1], {"coef": (c + 8 - j) % 8, "obs": o})

    for j in range(1, 5):
        table_copy(j).start()
    row_copy = copy(rows_l, rows_o, rows_s, rows_r, y_up)
    row_copy.start()
    whites = []
    for n, (block, way) in enumerate([(3, 0), (2, 1), (0, 0), (1, 1)]):
        area = (pl.ds(block * TILE, TILE), pl.ds(0, (block + 1) * TILE))
        whites.append(copy(white_ref.at[area], white_o.at[area], white_s.at[n], white_r.at[n],
                           y_up if way == 0 else y_down))
    for w in whites:
        w.start()

    parity = (lax.broadcasted_iota(jnp.int32, (8, SEG), 0) % 2).astype(F32)

    def triangular(operand, white, put):
        for block in range(SEG // TILE):
            depth = (block + 1) * TILE
            put(block, lax.dot_general(
                operand[:, :depth], white[pl.ds(block * TILE, TILE), pl.ds(0, depth)], NT,
                preferred_element_type=F32))

    def keep_level(level, value):
        for part in range(8):
            dscr[part, pl.ds(level, 8, stride=PITCH), :] = value[:, part * 128:(part + 1) * 128]

    def design(rows, d):
        coefs = tab[(here + d) % NSETS]
        order, log_const = coefs[:, 0:1], coefs[:, 64:65]
        sectorial = math.sqrt(2.0) * jnp.exp(log_const + order * rows[0:1, :])
        cosine = jnp.broadcast_to(rows[1:2, :], (8, SEG))
        turn = order * rows[2:3, :] - 0.25 * parity
        turn = turn - jnp.floor(turn + 0.5)
        square = turn * turn
        harmonic = jnp.full_like(square, COS_TERMS[-1])
        for term in COS_TERMS[-2::-1]:
            harmonic = harmonic * square + term
        lower = sectorial * harmonic
        lowest = jnp.zeros_like(lower)
        keep_level(0, lower)
        for level in range(1, LEV):
            value = (coefs[:, level:level + 1] * cosine) * lower - coefs[:, 64 + level:65 + level] * lowest
            keep_level(level, value)
            lower, lowest = value, lower
            if level % 8 == 7:
                yield
        for slot in range(8):
            for part in range(8):
                dbf[slot * LEV:(slot + 1) * LEV, part * 128:(part + 1) * 128] = (
                    dscr[part, slot * PITCH:slot * PITCH + LEV, :].astype(BF16))
            yield

    def whiten(white):
        for block in range(SEG // TILE):
            depth = (block + 1) * TILE
            value = lax.dot_general(
                dbf[:, :depth], white[block * TILE:(block + 1) * TILE, :depth], NT, preferred_element_type=F32)
            filt[:, block * TILE:(block + 1) * TILE] = value.astype(BF16)

    def make_whitened(rows, white):
        pieces = split_rows(rows[3:4, :])

        def put(block, value):
            row = jnp.sum(value, axis=0, keepdims=True)
            wv[:, block * TILE:(block + 1) * TILE] = split_rows(row)

        triangular(pieces, white, put)

    def rhs_terms():
        terms = lax.dot_general(wv[...], filt[...], NT, preferred_element_type=F32)
        return jnp.broadcast_to(jnp.sum(terms, axis=0, keepdims=True), (8, SET))

    order_z = [z, 3 - z, 3 - z_odd, z_odd]

    def keep_left(column):
        for half, kk in enumerate((1 - k, k)):
            for n, zz in enumerate(order_z):
                left[half * 256 + n * 64:half * 256 + n * 64 + 64, column:column + SEG] = (
                    filt[pl.ds(pl.multiple_of((2 * zz + kk) * 64, 64), 64), :])

    def product(n, column):
        return lax.dot_general(left[:, column:column + SEG], filt[n * 256:(n + 1) * 256, :], NT, preferred_element_type=F32)

    def own_terms(d):
        for n in range(2):
            part[d, :, n * 256:(n + 1) * 256] = product(n, 0)
            yield

    interleave(design(rows_l, 0))
    load.wait()
    make_whitened(rows_l, white_l)

    def own_stage(d, carry):
        whiten(white_l)

        @pl.when(d == 0)
        def _():
            keep_left(0)
            sR[0] = rhs_terms()

        for j in range(4):
            @pl.when(d == 2 * j)
            def _(j=j):
                table_copy(j + 1).wait()

        interleave(own_terms(d), design(rows_l, d + 1))
        return carry

    lax.fori_loop(0, NEAR - 1, own_stage, 0)
    whiten(white_l)
    row_copy.wait()
    interleave(own_terms(NEAR - 1), design(rows_o, 0))
    for w in whites:
        w.wait()
    make_whitened(rows_o, white_o)

    def rhs_copy(n):
        return copy(sR.at[n], rR.at[n], r_s.at[n], r_r.at[n], (sibling, z_first, z_second, y_pair)[n])

    def rhs_step(n):
        rhs_copy(n).wait()
        if n < 3:
            sR[n + 1] = sR[n] + rR[n]
            rhs_copy(n + 1).start()
        else:
            for zz in range(4):
                lanes = slice(zz * 128, (zz + 1) * 128)
                rhs_ref[0:1, pl.ds(pl.multiple_of(zz * 256 + y_lo * 128, 128), 128)] = sR[3, 0:1, lanes]
                rhs_ref[0:1, pl.ds(pl.multiple_of(zz * 256 + (1 - y_lo) * 128, 128), 128)] = rR[3, 0:1, lanes]

    inv_rows = 1.0 / (16.0 * SEG)

    def base_of(q):
        return (q // 2) * 1024 + (q % 2) * 128

    def k_copy(j):
        return copy(sK.at[j], rK.at[j], k_s.at[j], k_r.at[j], sibling)

    def z_copies(j):
        return [copy(sZ.at[j, h], rZ.at[j, h], z_s.at[j, h], z_r.at[j, h], (z_first, z_second)[h]) for h in range(2)]

    def y_copies(j):
        return [copy(sY.at[j, h], rY.at[j, h], y_s.at[j, h], y_r.at[j, h], (z_second, z_first)[h]) for h in range(2)]

    def t_copy(j, slot):
        q = (here + j + 1) % NSETS
        return copy(sT.at[j, slot], rT.at[j, 2 * z + k], t_s.at[j, slot], t_r.at[j],
                    at(q // 4, q % 4, slot // 2, slot % 2))

    def finish(j):
        for move in y_copies(j):
            move.wait_recv()
        total = inv_rows * (tot[j % 2] + jnp.concatenate([rY[j, 0], rY[j, 1]], axis=1).astype(F32))
        base = base_of((here + j) % NSETS)
        for zz in range(4):
            out_ref[:, pl.ds(pl.multiple_of(base + zz * 256, 128), 128)] = total[:, zz * 128:(zz + 1) * 128]

        def mirror():
            turned = total.T
            for slot in range(8):
                sT[j - 1, slot] = jnp.concatenate(
                    [turned[slot * 64:slot * 64 + 32], turned[slot * 64 + 32:slot * 64 + 64]], axis=1).astype(BF16)

            def send(slot, carry):
                t_copy(j - 1, slot).start()
                return carry

            lax.fori_loop(0, 8, send, 0)

        if isinstance(j, int):
            if 1 <= j <= MIRROR:
                mirror()
        else:
            pl.when(j >= 1)(mirror)

    def second(j):
        par = j % 2
        for move in z_copies(j):
            move.wait_recv()
        sY[j, 0] = (keepA[par, 64:128, :] + rZ[j, 0, 0:64, :].astype(F32)).astype(BF16)
        sY[j, 1] = (keepB[par, 64:128, :] + rZ[j, 1, 64:128, :].astype(F32)).astype(BF16)
        for move in y_copies(j):
            move.start()
        tot[par, :, 0:256] = keepA[par, 0:64, :] + rZ[j, 0, 64:128, :].astype(F32)
        tot[par, :, 256:512] = keepB[par, 0:64, :] + rZ[j, 1, 0:64, :].astype(F32)

    def third(j):
        par = j % 2
        k_copy(j).wait_recv()
        sZ[j, 0] = (own[par, 128:256, 0:256] + rK[j, 128:256, 0:256].astype(F32)).astype(BF16)
        sZ[j, 1] = (own[par, 64:192, 256:512] + rK[j, 64:192, 256:512].astype(F32)).astype(BF16)
        for move in z_copies(j):
            move.start()
        keepA[par] = own[par, 0:128, 0:256] + rK[j, 0:128, 0:256].astype(F32)
        keepB[par, 0:64, :] = own[par, 0:64, 256:512] + rK[j, 0:64, 256:512].astype(F32)
        keepB[par, 64:128, :] = own[par, 192:256, 256:512] + rK[j, 192:256, 256:512].astype(F32)

    def gram(j):
        for n in range(2):
            lanes = slice(n * 256, (n + 1) * 256)
            total = part[j, :, lanes] + product(n, SEG)
            sK[j, :, lanes] = total[0:256].astype(BF16)
            own[j % 2, :, lanes] = total[256:512]
            yield

    def mirrored(j, carry):
        copy(sT.at[j], rT.at[j], t_s.at[j, 0], t_r.at[j], sibling).wait_recv()
        base = base_of((here + NSETS - 1 - j) % NSETS)
        for zz in range(4):
            for half in range(2):
                lanes = slice(half * 64, half * 64 + 64)
                piece = jnp.concatenate(
                    [rT[j, 2 * zz, :, lanes].astype(F32), rT[j, 2 * zz + 1, :, lanes].astype(F32)], axis=1)
                out_ref[half * 32:half * 32 + 32, pl.ds(pl.multiple_of(base + zz * 256, 128), 128)] = piece

        def sent(slot, inner):
            t_copy(j, slot).wait_send()
            return inner

        lax.fori_loop(0, 8, sent, 0)
        return carry

    def stage(i, carry):
        whiten(white_o)

        @pl.when(i == 0)
        def _():
            keep_left(SEG)
            sR[0] = sR[0] + rhs_terms()
            rhs_copy(0).start()

        for n in range(4):
            @pl.when(i == n + 1)
            def _(n=n):
                rhs_step(n)

        @pl.when(i >= 1)
        def _():
            third(i - 1)

        @pl.when(i >= 2)
        def _():
            second(i - 2)

        @pl.when(i >= 3)
        def _():
            finish(i - 3)

        interleave(gram(i), design(rows_o, jnp.minimum(i + 1, NEAR - 1)))
        k_copy(i).start()
        return carry

    lax.fori_loop(0, NEAR, stage, 0)
    third(8)
    second(7)
    finish(6)
    lax.fori_loop(0, 3, mirrored, 0)
    second(8)
    finish(7)
    lax.fori_loop(3, 5, mirrored, 0)
    finish(8)
    lax.fori_loop(5, MIRROR, mirrored, 0)


    def drain(j, carry):
        k_copy(j).wait_send()
        for move in z_copies(j) + y_copies(j):
            move.wait_send()
        return carry

    lax.fori_loop(0, NEAR, drain, 0)


def hand_over(normal_ref, rhs_ref, normal_out, rhs_out, sems):
    moves = [
        pltpu.make_async_copy(normal_ref.at[pl.ds(n * 16, 16)], normal_out.at[pl.ds(n * 16, 16)], sems.at[n])
        for n in range(4)
    ]
    for move in moves:
        move.start()
    rhs_out[...] = rhs_ref[...] * (1.0 / math.sqrt(16.0 * SEG))
    for move in moves:
        move.wait()


def on_device(sample_index, colatitude, longitude, orders, observed, whitening):
    vmem = pl.BlockSpec(memory_space=pltpu.VMEM)
    V = pltpu.VMEM
    dma = pltpu.SemaphoreType.DMA
    normal, rhs = pl.pallas_call(
        main_kernel,
        out_shape=(jax.ShapeDtypeStruct((64, 8192), F32), jax.ShapeDtypeStruct((1, SEG), F32)),
        in_specs=[vmem] * 5 + [pl.BlockSpec(memory_space=pl.ANY)],
        out_specs=(vmem, vmem),
        scratch_shapes=[
            V((NSETS, 8, 128), F32), V((8, SEG), F32), V((8, SEG), F32),
            V((SEG, SEG), BF16), V((SEG, SEG), BF16),
            V((8, 8 * PITCH, 128), F32), V((SET, SEG), BF16), V((SET, SEG), BF16),
            V((NEAR, SET, SET), F32),
            V((SET, 2 * SEG), BF16), V((16, SEG), BF16), V((2, 256, SET), F32),
            V((NEAR, 256, SET), BF16), V((NEAR, 256, SET), BF16),
            V((NEAR, 2, 128, 256), BF16), V((NEAR, 2, 128, 256), BF16),
            V((NEAR, 2, 64, 256), BF16), V((NEAR, 2, 64, 256), BF16),
            V((2, 128, 256), F32), V((2, 128, 256), F32), V((2, 64, SET), F32),
            V((MIRROR, 8, 32, 128), BF16), V((MIRROR, 8, 32, 128), BF16),
            V((4, 8, SET), F32), V((4, 8, SET), F32),
            dma, dma((4,)), dma((4,)), dma, dma, dma((4,)), dma((4,)),
            dma((NEAR,)), dma((NEAR,)), dma((NEAR, 2)), dma((NEAR, 2)),
            dma((NEAR, 2)), dma((NEAR, 2)), dma((MIRROR, 8)), dma((MIRROR,)),
            dma((4,)), dma((4,)),
        ],
        compiler_params=pltpu.CompilerParams(
            collective_id=0, has_side_effects=True, vmem_limit_bytes=60 * 2**20,
        ),
    )(
        sample_index.reshape(1, SEG), colatitude.reshape(128, 128), longitude.reshape(128, 128),
        orders.reshape(1, 16), observed.reshape(1, SEG), whitening,
    )
    hbm = pl.BlockSpec(memory_space=pl.ANY)
    normal, rhs = pl.pallas_call(
        hand_over,
        out_shape=(jax.ShapeDtypeStruct((64, 8192), F32), jax.ShapeDtypeStruct((1, SEG), F32)),
        in_specs=[hbm, vmem],
        out_specs=(hbm, vmem),
        scratch_shapes=[dma((4,))],
    )(normal, rhs)
    return normal, rhs.reshape(SEG)


def solution(mesh):
    placed = (P("obs"), P(), P(), P("coef"), P("obs"), P("obs", None))
    return jax.shard_map(
        on_device,
        mesh=mesh,
        in_specs=placed,
        out_specs=(P(("coef", "obs"), None), P("coef")),
        check_vma=False,
    )
```

```python
import functools
import math

import jax
import jax.numpy as jnp
from jax import lax
from jax.experimental import pallas as pl
from jax.experimental.pallas import tpu as pltpu
from jax.sharding import PartitionSpec as P

LEV = 64
NMAX = 300
SEG = 1024
SET = 512
NSETS = 16
NEAR = 9
MIRROR = 7
TILE = 256
PITCH = 65
F32 = jnp.float32
BF16 = jnp.bfloat16
MESH = pl.DeviceIdType.MESH
NT = (((1,), (1,)), ((), ()))
COS_TERMS = [(-1.0) ** i * (2.0 * math.pi) ** (2 * i) / math.factorial(2 * i) for i in range(11)]


def prepare(index_ref, colat_ref, long_ref, observed_ref, rows_ref):
    index = index_ref[...]
    high, low = index // 128, index % 128
    pos = lax.broadcasted_iota(jnp.int32, (128, SEG), 0)
    pick_high = (pos == high).astype(F32)
    pick_low = (pos == low).astype(F32)

    def look_up(table):
        found = lax.dot_general(
            table, pick_high, (((0,), (0,)), ((), ())),
            precision=lax.Precision.HIGHEST, preferred_element_type=F32,
        )
        return jnp.sum(found * pick_low, axis=0, keepdims=True)

    colat = look_up(colat_ref[...])
    longitude = look_up(long_ref[...])
    rows_ref[...] = jnp.zeros(rows_ref.shape, F32)
    rows_ref[0:1, :] = jnp.log(jnp.sin(colat))
    rows_ref[1:2, :] = jnp.cos(colat)
    rows_ref[2:3, :] = longitude * (0.5 / math.pi)
    rows_ref[3:4, :] = observed_ref[...]


def make_table(orders_ref):
    place = lax.broadcasted_iota(jnp.int32, (16, 16), 0)
    wanted = (place // 2 % 4) * 4 + (place // 8) * 2 + place % 2
    given = lax.broadcasted_iota(jnp.int32, (16, 16), 1)
    order = jnp.sum(jnp.where(given == wanted, orders_ref[...].astype(F32), 0.0), axis=1, keepdims=True)
    counter = (lax.broadcasted_iota(jnp.int32, (16, 384), 1) + 1).astype(F32)
    log_const = jnp.sum(
        jnp.where(counter <= order, 0.5 * jnp.log((2.0 * counter + 1.0) / (2.0 * counter)), 0.0),
        axis=1, keepdims=True,
    )
    lane = lax.broadcasted_iota(jnp.int32, (16, 128), 1)
    step = jnp.maximum(lane % 64, 1).astype(F32)
    degree = order + step
    rise = jnp.sqrt((2.0 * degree - 1.0) * (2.0 * degree + 1.0) / (step * (degree + order)))
    fall = jnp.sqrt(
        (2.0 * degree + 1.0) * (degree + order - 1.0) * (step - 1.0)
        / ((2.0 * degree - 3.0) * (degree + order) * step)
    )
    table = jnp.where(lane < 64, rise, fall)
    table = jnp.where(lane == 0, order, table)
    return jnp.where(lane == 64, log_const, table)


def in_turn(*parts):
    for part in parts:
        yield from part


def chip_of(q):
    high, low = q // 4, q % 4
    return (high + 2 * low) % 4, (high + 3 * low) % 4


def set_of(j):
    return 8 - (j + 1) % 8


def interleave(*parts):
    parts = list(parts)
    while parts:
        for part in list(parts):
            try:
                next(part)
            except StopIteration:
                parts.remove(part)


def split_rows(row):
    high = row.astype(BF16).astype(F32)
    rest = row - high
    middle = rest.astype(BF16).astype(F32)
    low = rest - middle
    place = lax.broadcasted_iota(jnp.int32, (16, row.shape[1]), 0)
    pieces = jnp.where(place == 0, high, jnp.where(place == 1, middle, jnp.where(place == 2, low, 0.0)))
    return pieces.astype(BF16)


def main_kernel(
    index_ref, colat_ref, long_ref, orders_ref, observed_ref, white_ref, out_ref, rhs_ref,
    tab, rows_l, rows_o, white_l, white_o, dscr, dbf, dbf0, filt, filt0, part, left, wv, own,
    sK, rK, sZ, rZ, sY, rY, keepA, keepB, keepD, tot, sD, rD, sT, rT, sR, rR,
    load_s, table_s, table_r, rows_s, rows_r, white_s, white_r,
    k_s, k_r, z_s, z_r, y_s, y_r, d_s, d_r, t_s, t_r, r_s, r_r,
):
    c, o = lax.axis_index("coef"), lax.axis_index("obs")
    x, y_hi = c // 2, c % 2
    z, y_lo, k = o // 4, (o // 2) % 2, o % 2
    y = 2 * y_hi + y_lo
    low = (y - x + 4) % 4
    here = 4 * ((x + 8 - 2 * low) % 4) + low

    def at(xx, yy, zz, kk):
        return {"coef": 2 * xx + yy // 2, "obs": 4 * zz + 2 * (yy % 2) + kk}

    z_odd = z + 1 - 2 * (z % 2)
    sibling = at(x, y, z, 1 - k)
    z_first = at(x, y, z_odd, k)
    z_second = at(x, y, 3 - z, k)
    y_up = at(x, (y + 1) % 4, z, k)
    y_down = at(x, (y + 3) % 4, z, k)
    y_pair = at(x, y + 1 - 2 * y_lo, z, k)
    z_far = at(x, y, (z + 2) % 4, k)
    near = [sibling, z_first, z_second, z_far, y_up, y_down]
    near += [{"coef": (c + j) % 8, "obs": o} for j in range(1, 8)]

    def copy(src, dst, send, recv, device):
        return pltpu.make_async_remote_copy(
            src_ref=src, dst_ref=dst, send_sem=send, recv_sem=recv,
            device_id=device, device_id_type=MESH,
        )

    barrier = pltpu.get_barrier_semaphore()
    for device in near:
        pl.semaphore_signal(barrier, inc=1, device_id=device, device_id_type=MESH)
    load = pltpu.make_async_copy(white_ref, white_l, load_s)
    load.start()
    table = make_table(orders_ref)
    tab[2 * c] = table[0:8]
    tab[2 * c + 1] = table[8:16]
    pl.semaphore_wait(barrier, len(near))

    def table_copy(j):
        mine = tab.at[pl.ds(2 * c, 2)]
        return copy(mine, mine, table_s.at[j - 1], table_r.at[j - 1], {"coef": (c + 8 - j) % 8, "obs": o})

    for j in range(1, 8):
        table_copy(j).start()
    whites = []
    for n, (block, way) in enumerate([(7, 0), (5, 1), (6, 0), (4, 1), (2, 0), (3, 1), (1, 1), (0, 1)]):
        area = (pl.ds(block * 128, 128), pl.ds(0, (block + 1) * 128))
        whites.append(copy(white_ref.at[area], white_o.at[area], white_s.at[n], white_r.at[n],
                           y_up if way == 0 else y_down))
    for w in whites:
        w.start()
    prepare(index_ref, colat_ref, long_ref, observed_ref, rows_l)
    row_copy = copy(rows_l, rows_o, rows_s, rows_r, y_up)
    row_copy.start()

    for block in range(4):
        white_o[block * TILE:block * TILE + 128, block * TILE + 128:(block + 1) * TILE] = jnp.zeros((128, 128), BF16)
    parity = (lax.broadcasted_iota(jnp.int32, (8, SEG), 0) % 2).astype(F32)

    def triangular(operand, white, put):
        for block in range(SEG // TILE):
            depth = (block + 1) * TILE
            put(block, lax.dot_general(
                operand[:, :depth], white[pl.ds(block * TILE, TILE), pl.ds(0, depth)], NT,
                preferred_element_type=F32))

    def keep_level(level, value):
        for part in range(8):
            dscr[part, pl.ds(level, 8, stride=PITCH), :] = value[:, part * 128:(part + 1) * 128]

    def design(rows, d, dst):
        set_x, set_y = chip_of((here + d) % NSETS)
        coefs = tab[4 * set_x + set_y]
        order, log_const = coefs[:, 0:1], coefs[:, 64:65]
        sectorial = math.sqrt(2.0) * jnp.exp(log_const + order * rows[0:1, :])
        cosine = jnp.broadcast_to(rows[1:2, :], (8, SEG))
        turn = order * rows[2:3, :] - 0.25 * parity
        turn = turn - jnp.floor(turn + 0.5)
        square = turn * turn
        harmonic = jnp.full_like(square, COS_TERMS[-1])
        for term in COS_TERMS[-2::-1]:
            harmonic = harmonic * square + term
        lower = sectorial * harmonic
        lowest = jnp.zeros_like(lower)
        keep_level(0, lower)
        for level in range(1, LEV):
            value = (coefs[:, level:level + 1] * cosine) * lower - coefs[:, 64 + level:65 + level] * lowest
            keep_level(level, value)
            lower, lowest = value, lower
            if level % 8 == 7:
                yield
        for slot in range(8):
            for part in range(8):
                dst[slot * LEV:(slot + 1) * LEV, part * 128:(part + 1) * 128] = (
                    dscr[part, slot * PITCH:slot * PITCH + LEV, :].astype(BF16))
            yield

    def whiten(white, src, dst):
        for block in range(SEG // TILE):
            depth = (block + 1) * TILE
            value = lax.dot_general(
                src[:, :depth], white[block * TILE:(block + 1) * TILE, :depth], NT, preferred_element_type=F32)
            dst[:, block * TILE:(block + 1) * TILE] = value.astype(BF16)

    def make_whitened(rows, white):
        pieces = split_rows(rows[3:4, :])

        def put(block, value):
            row = jnp.sum(value, axis=0, keepdims=True)
            wv[:, block * TILE:(block + 1) * TILE] = split_rows(row)

        triangular(pieces, white, put)

    def rhs_terms(src):
        terms = lax.dot_general(wv[...], src[...], NT, preferred_element_type=F32)
        return jnp.broadcast_to(jnp.sum(terms, axis=0, keepdims=True), (8, SET))

    order_z = [z, 3 - z, 3 - z_odd, z_odd]

    def keep_left(src, column):
        for half, kk in enumerate((1 - k, k)):
            for n, zz in enumerate(order_z):
                left[half * 256 + n * 64:half * 256 + n * 64 + 64, column:column + SEG] = (
                    src[pl.ds(pl.multiple_of((2 * zz + kk) * 64, 64), 64), :])

    def product(n, column, src):
        return lax.dot_general(left[:, column:column + SEG], src[n * 256:(n + 1) * 256, :], NT, preferred_element_type=F32)

    def own_terms(d):
        for n in range(2):
            part[d, :, n * 256:(n + 1) * 256] = product(n, 0, filt)
            yield

    interleave(design(rows_l, 0, dbf))
    load.wait()
    make_whitened(rows_l, white_l)

    def own_stage(d, carry):
        whiten(white_l, dbf, filt)

        @pl.when(d == 0)
        def _():
            keep_left(filt, 0)
            sR[0] = rhs_terms(filt)

        @pl.when(d == 0)
        def _():
            for j in range(1, 8):
                table_copy(j).wait()

        interleave(own_terms(d), design(rows_l, d + 1, dbf))
        return carry

    lax.fori_loop(0, NEAR - 1, own_stage, 0)
    whiten(white_l, dbf, filt)
    row_copy.wait()
    interleave(own_terms(NEAR - 1), in_turn(design(rows_o, 0, dbf0), design(rows_o, set_of(0), dbf)))
    for w in whites:
        w.wait()
    whiten(white_o, dbf0, filt0)
    make_whitened(rows_o, white_o)
    keep_left(filt0, SEG)

    def rhs_copy(n):
        return copy(sR.at[n], rR.at[n], r_s.at[n], r_r.at[n], (sibling, z_first, z_second, y_pair)[n])

    def rhs_step(n):
        rhs_copy(n).wait()
        if n < 3:
            sR[n + 1] = sR[n] + rR[n]
            rhs_copy(n + 1).start()
        else:
            for zz in range(4):
                lanes = slice(zz * 128, (zz + 1) * 128)
                rhs_ref[0:1, pl.ds(pl.multiple_of(zz * 256 + y_lo * 128, 128), 128)] = sR[3, 0:1, lanes]
                rhs_ref[0:1, pl.ds(pl.multiple_of(zz * 256 + (1 - y_lo) * 128, 128), 128)] = rR[3, 0:1, lanes]

    def base_of(q):
        set_x, set_y = chip_of(q)
        return (2 * set_x + set_y // 2) * 1024 + (set_y % 2) * 128

    def k_copy(j):
        return copy(sK.at[j], rK.at[j], k_s.at[j], k_r.at[j], sibling)

    def z_copies(j):
        return [copy(sZ.at[j, h], rZ.at[j, h], z_s.at[j, h], z_r.at[j, h], (z_first, z_second)[h]) for h in range(2)]

    def y_copies(j):
        return [copy(sY.at[j, h], rY.at[j, h], y_s.at[j, h], y_r.at[j, h], (z_second, z_first)[h]) for h in range(2)]

    def t_copy(j, slot):
        q = (here + set_of(j)) % NSETS
        return copy(sT.at[j, slot], rT.at[j, 2 * z + k], t_s.at[j, slot], t_r.at[j],
                    at(*chip_of(q), slot // 2, slot % 2))

    def far_copies():
        return [copy(sD.at[h], rD.at[h], d_s.at[h], d_r.at[h], (z_second, z_far, z_first)[h]) for h in range(3)]

    def emit(total, d):
        base = base_of((here + d) % NSETS)
        for zz in range(4):
            out_ref[:, pl.ds(pl.multiple_of(base + zz * 256, 128), 128)] = total[:, zz * 128:(zz + 1) * 128]

    def mirror(j, total):
        turned = total.T
        for slot in range(8):
            sT[j, slot] = jnp.concatenate(
                [turned[slot * 64:slot * 64 + 32], turned[slot * 64 + 32:slot * 64 + 64]], axis=1).astype(BF16)

        def send(slot, carry):
            t_copy(j, slot).start()
            return carry

        lax.fori_loop(0, 8, send, 0)

    def finish(j):
        for move in y_copies(j):
            move.wait_recv()
        total = (tot[j % 4] + jnp.concatenate([rY[j, 0], rY[j, 1]], axis=1).astype(F32))
        if not isinstance(j, int) or j < MIRROR:
            mirror(j, total)
        emit(total, 0 if isinstance(j, int) and j == 8 else set_of(j))

    def finish_far():
        for move in far_copies():
            move.wait_recv()
        total = keepD[...] + rD[0].astype(F32) + rD[1].astype(F32) + rD[2].astype(F32)
        mirror(6, total)
        emit(total, 1)

    def third_far():
        k_copy(6).wait_recv()
        for h in range(3):
            rows = slice(64 * (h + 1), 64 * (h + 2))
            sD[h] = (own[0, rows, :] + rK[6, rows, :].astype(F32)).astype(BF16)
        for move in far_copies():
            move.start()
        keepD[...] = own[0, 0:64, :] + rK[6, 0:64, :].astype(F32)

    def second(j):
        par = j % 4
        for move in z_copies(j):
            move.wait_recv()
        sY[j, 0] = (keepA[par, 64:128, :] + rZ[j, 0, 0:64, :].astype(F32)).astype(BF16)
        sY[j, 1] = (keepB[par, 64:128, :] + rZ[j, 1, 64:128, :].astype(F32)).astype(BF16)
        for move in y_copies(j):
            move.start()
        tot[par, :, 0:256] = keepA[par, 0:64, :] + rZ[j, 0, 64:128, :].astype(F32)
        tot[par, :, 256:512] = keepB[par, 0:64, :] + rZ[j, 1, 0:64, :].astype(F32)

    def third(j):
        par, now = j % 4, j % 2
        k_copy(j).wait_recv()
        sZ[j, 0] = (own[now, 128:256, 0:256] + rK[j, 128:256, 0:256].astype(F32)).astype(BF16)
        sZ[j, 1] = (own[now, 64:192, 256:512] + rK[j, 64:192, 256:512].astype(F32)).astype(BF16)
        for move in z_copies(j):
            move.start()
        keepA[par] = own[now, 0:128, 0:256] + rK[j, 0:128, 0:256].astype(F32)
        keepB[par, 0:64, :] = own[now, 0:64, 256:512] + rK[j, 0:64, 256:512].astype(F32)
        keepB[par, 64:128, :] = own[now, 192:256, 256:512] + rK[j, 192:256, 256:512].astype(F32)

    def gram(j, d, src):
        for n in range(2):
            lanes = slice(n * 256, (n + 1) * 256)
            total = part[d, :, lanes] + product(n, SEG, src)
            sK[j, :, lanes] = total[0:256].astype(BF16)
            own[j % 2, :, lanes] = total[256:512]
            yield

    def mirrored(j, carry):
        copy(sT.at[j], rT.at[j], t_s.at[j, 0], t_r.at[j], sibling).wait_recv()
        base = base_of((here + NSETS - set_of(j)) % NSETS)
        for zz in range(4):
            for half in range(2):
                lanes = slice(half * 64, half * 64 + 64)
                piece = jnp.concatenate(
                    [rT[j, 2 * zz, :, lanes].astype(F32), rT[j, 2 * zz + 1, :, lanes].astype(F32)], axis=1)
                out_ref[half * 32:half * 32 + 32, pl.ds(pl.multiple_of(base + zz * 256, 128), 128)] = piece

        def sent(slot, inner):
            t_copy(j, slot).wait_send()
            return inner

        lax.fori_loop(0, 8, sent, 0)
        return carry

    sR[0] = sR[0] + rhs_terms(filt0)
    rhs_copy(0).start()

    def stage(i, carry):
        @pl.when(i >= 2)
        def _():
            third(i - 2)

        for n in range(4):
            @pl.when(i == 2 * n + 1)
            def _(n=n):
                rhs_step(n)

        @pl.when(i >= 7)
        def _():
            finish(i - 7)

        whiten(white_o, dbf, filt)

        @pl.when(i >= 4)
        def _():
            second(i - 4)

        interleave(gram(i, set_of(i), filt), design(rows_o, set_of(jnp.minimum(i + 1, 7)), dbf))
        k_copy(i).start()
        return carry

    lax.fori_loop(0, 8, stage, 0)
    third_far()
    finish(1)
    interleave(gram(8, 0, filt0))
    k_copy(8).start()
    second(4)
    third(7)
    finish(2)
    third(8)
    second(5)
    finish(3)
    finish_far()
    finish(4)
    second(7)
    lax.fori_loop(0, 1, mirrored, 0)
    finish(5)
    second(8)
    lax.fori_loop(1, 3, mirrored, 0)
    finish(7)
    lax.fori_loop(3, 4, mirrored, 0)
    finish(8)
    lax.fori_loop(4, MIRROR, mirrored, 0)

    def drain(j, carry):
        k_copy(j).wait_send()
        return carry

    lax.fori_loop(0, NEAR, drain, 0)

    def drain_z(j, carry):
        for move in z_copies(j) + y_copies(j):
            move.wait_send()
        return carry

    lax.fori_loop(0, 6, drain_z, 0)
    lax.fori_loop(7, 9, drain_z, 0)
    for move in far_copies():
        move.wait_send()


def on_device(sample_index, colatitude, longitude, orders, observed, whitening):
    vmem = pl.BlockSpec(memory_space=pltpu.VMEM)
    V = pltpu.VMEM
    dma = pltpu.SemaphoreType.DMA
    normal, rhs = pl.pallas_call(
        main_kernel,
        out_shape=(jax.ShapeDtypeStruct((64, 8192), F32), jax.ShapeDtypeStruct((1, SEG), F32)),
        in_specs=[vmem] * 5 + [pl.BlockSpec(memory_space=pl.ANY)],
        out_specs=(vmem, vmem),
        scratch_shapes=[
            V((NSETS, 8, 128), F32), V((8, SEG), F32), V((8, SEG), F32),
            V((SEG, SEG), BF16), V((SEG, SEG), BF16),
            V((8, 8 * PITCH, 128), F32), V((SET, SEG), BF16), V((SET, SEG), BF16), V((SET, SEG), BF16), V((SET, SEG), BF16),
            V((NEAR, SET, SET), F32),
            V((SET, 2 * SEG), BF16), V((16, SEG), BF16), V((2, 256, SET), F32),
            V((NEAR, 256, SET), BF16), V((NEAR, 256, SET), BF16),
            V((NEAR, 2, 128, 256), BF16), V((NEAR, 2, 128, 256), BF16),
            V((NEAR, 2, 64, 256), BF16), V((NEAR, 2, 64, 256), BF16),
            V((4, 128, 256), F32), V((4, 128, 256), F32), V((64, SET), F32), V((4, 64, SET), F32),
            V((3, 64, SET), BF16), V((3, 64, SET), BF16),
            V((MIRROR, 8, 32, 128), BF16), V((MIRROR, 8, 32, 128), BF16),
            V((4, 8, SET), F32), V((4, 8, SET), F32),
            dma, dma((7,)), dma((7,)), dma, dma, dma((8,)), dma((8,)),
            dma((NEAR,)), dma((NEAR,)), dma((NEAR, 2)), dma((NEAR, 2)),
            dma((NEAR, 2)), dma((NEAR, 2)), dma((3,)), dma((3,)), dma((MIRROR, 8)), dma((MIRROR,)),
            dma((4,)), dma((4,)),
        ],
        compiler_params=pltpu.CompilerParams(
            collective_id=0, has_side_effects=True, vmem_limit_bytes=60 * 2**20,
        ),
    )(
        sample_index.reshape(1, SEG), colatitude.reshape(128, 128), longitude.reshape(128, 128),
        orders.reshape(1, 16), observed.reshape(1, SEG), whitening,
    )
    rows = 16.0 * SEG
    return normal * (1.0 / rows), rhs.reshape(SEG) * (1.0 / math.sqrt(rows))


def solution(mesh):
    placed = (P("obs"), P(), P(), P("coef"), P("obs"), P("obs", None))
    return jax.shard_map(
        on_device,
        mesh=mesh,
        in_specs=placed,
        out_specs=(P(("coef", "obs"), None), P("coef")),
        check_vma=False,
    )
```

```python
import functools
import math

import jax
import jax.numpy as jnp
from jax import lax
from jax.experimental import pallas as pl
from jax.experimental.pallas import tpu as pltpu
from jax.sharding import PartitionSpec as P

LEV = 64
NMAX = 300
SEG = 1024
SET = 512
NSETS = 16
NEAR = 9
MIRROR = 7
TILE = 256
PITCH = 65
F32 = jnp.float32
BF16 = jnp.bfloat16
MESH = pl.DeviceIdType.MESH
NT = (((1,), (1,)), ((), ()))
COS_TERMS = [(-1.0) ** i * (2.0 * math.pi) ** (2 * i) / math.factorial(2 * i) for i in range(11)]


def prepare(index_ref, colat_ref, long_ref, observed_ref, rows_ref):
    index = index_ref[...]
    high, low = index // 128, index % 128
    pos = lax.broadcasted_iota(jnp.int32, (128, SEG), 0)
    pick_high = (pos == high).astype(F32)
    pick_low = (pos == low).astype(F32)

    def look_up(table):
        found = lax.dot_general(
            table, pick_high, (((0,), (0,)), ((), ())),
            precision=lax.Precision.HIGHEST, preferred_element_type=F32,
        )
        return jnp.sum(found * pick_low, axis=0, keepdims=True)

    colat = look_up(colat_ref[...])
    longitude = look_up(long_ref[...])
    rows_ref[...] = jnp.zeros(rows_ref.shape, F32)
    rows_ref[0:1, :] = jnp.log(jnp.sin(colat))
    rows_ref[1:2, :] = jnp.cos(colat)
    rows_ref[2:3, :] = longitude * (0.5 / math.pi)
    rows_ref[3:4, :] = observed_ref[...]


def make_table(orders_ref):
    place = lax.broadcasted_iota(jnp.int32, (16, 16), 0)
    wanted = (place // 2 % 4) * 4 + (place // 8) * 2 + place % 2
    given = lax.broadcasted_iota(jnp.int32, (16, 16), 1)
    order = jnp.sum(jnp.where(given == wanted, orders_ref[...].astype(F32), 0.0), axis=1, keepdims=True)
    counter = (lax.broadcasted_iota(jnp.int32, (16, 384), 1) + 1).astype(F32)
    log_const = jnp.sum(
        jnp.where(counter <= order, 0.5 * jnp.log((2.0 * counter + 1.0) / (2.0 * counter)), 0.0),
        axis=1, keepdims=True,
    )
    lane = lax.broadcasted_iota(jnp.int32, (16, 128), 1)
    step = jnp.maximum(lane % 64, 1).astype(F32)
    degree = order + step
    rise = jnp.sqrt((2.0 * degree - 1.0) * (2.0 * degree + 1.0) / (step * (degree + order)))
    fall = jnp.sqrt(
        (2.0 * degree + 1.0) * (degree + order - 1.0) * (step - 1.0)
        / ((2.0 * degree - 3.0) * (degree + order) * step)
    )
    table = jnp.where(lane < 64, rise, fall)
    table = jnp.where(lane == 0, order, table)
    return jnp.where(lane == 64, log_const, table)


def in_turn(*parts):
    for part in parts:
        yield from part


def chip_of(q):
    high, low = q // 4, q % 4
    return (high + 2 * low) % 4, (high + 3 * low) % 4


def set_of(j):
    return 8 - (j + 1) % 8


def interleave(*parts):
    parts = list(parts)
    while parts:
        for part in list(parts):
            try:
                next(part)
            except StopIteration:
                parts.remove(part)


def split_rows(row):
    high = row.astype(BF16).astype(F32)
    rest = row - high
    middle = rest.astype(BF16).astype(F32)
    low = rest - middle
    place = lax.broadcasted_iota(jnp.int32, (16, row.shape[1]), 0)
    pieces = jnp.where(place == 0, high, jnp.where(place == 1, middle, jnp.where(place == 2, low, 0.0)))
    return pieces.astype(BF16)


def main_kernel(
    index_ref, colat_ref, long_ref, orders_ref, observed_ref, white_ref, out_ref, rhs_ref,
    tab, rows_l, rows_o, white_l, white_o, dscr, dbf, dbf0, filt, filt0, part, left, wv, own,
    sK, rK, sZ, rZ, sY, rY, keepA, keepB, tot, sT, rT, sR, rR,
    load_s, table_s, table_r, rows_s, rows_r, white_s, white_r,
    k_s, k_r, z_s, z_r, y_s, y_r, t_s, t_r, r_s, r_r,
):
    c, o = lax.axis_index("coef"), lax.axis_index("obs")
    x, y_hi = c // 2, c % 2
    z, y_lo, k = o // 4, (o // 2) % 2, o % 2
    y = 2 * y_hi + y_lo
    low = (y - x + 4) % 4
    here = 4 * ((x + 8 - 2 * low) % 4) + low

    def at(xx, yy, zz, kk):
        return {"coef": 2 * xx + yy // 2, "obs": 4 * zz + 2 * (yy % 2) + kk}

    z_odd = z + 1 - 2 * (z % 2)
    sibling = at(x, y, z, 1 - k)
    z_first = at(x, y, z_odd, k)
    z_second = at(x, y, 3 - z, k)
    y_up = at(x, (y + 1) % 4, z, k)
    y_down = at(x, (y + 3) % 4, z, k)
    y_pair = at(x, y + 1 - 2 * y_lo, z, k)
    near = [sibling, z_first, z_second, y_up, y_down]
    near += [{"coef": (c + j) % 8, "obs": o} for j in range(1, 8)]

    def copy(src, dst, send, recv, device):
        return pltpu.make_async_remote_copy(
            src_ref=src, dst_ref=dst, send_sem=send, recv_sem=recv,
            device_id=device, device_id_type=MESH,
        )

    barrier = pltpu.get_barrier_semaphore()
    for device in near:
        pl.semaphore_signal(barrier, inc=1, device_id=device, device_id_type=MESH)
    load = pltpu.make_async_copy(white_ref, white_l, load_s)
    load.start()
    table = make_table(orders_ref)
    tab[2 * c] = table[0:8]
    tab[2 * c + 1] = table[8:16]
    pl.semaphore_wait(barrier, len(near))

    def table_copy(j):
        mine = tab.at[pl.ds(2 * c, 2)]
        return copy(mine, mine, table_s.at[j - 1], table_r.at[j - 1], {"coef": (c + 8 - j) % 8, "obs": o})

    for j in range(1, 8):
        table_copy(j).start()
    whites = []
    for n, (block, way) in enumerate([(7, 0), (5, 1), (6, 0), (4, 1), (2, 0), (3, 1), (1, 1), (0, 1)]):
        area = (pl.ds(block * 128, 128), pl.ds(0, (block + 1) * 128))
        whites.append(copy(white_ref.at[area], white_o.at[area], white_s.at[n], white_r.at[n],
                           y_up if way == 0 else y_down))
    for w in whites:
        w.start()
    prepare(index_ref, colat_ref, long_ref, observed_ref, rows_l)
    row_copy = copy(rows_l, rows_o, rows_s, rows_r, y_up)
    row_copy.start()

    for block in range(4):
        white_o[block * TILE:block * TILE + 128, block * TILE + 128:(block + 1) * TILE] = jnp.zeros((128, 128), BF16)
    parity = (lax.broadcasted_iota(jnp.int32, (8, SEG), 0) % 2).astype(F32)

    def triangular(operand, white, put):
        for block in range(SEG // TILE):
            depth = (block + 1) * TILE
            put(block, lax.dot_general(
                operand[:, :depth], white[pl.ds(block * TILE, TILE), pl.ds(0, depth)], NT,
                preferred_element_type=F32))

    def keep_level(level, value):
        for part in range(8):
            dscr[part, pl.ds(level, 8, stride=PITCH), :] = value[:, part * 128:(part + 1) * 128]

    def design(rows, d, dst):
        set_x, set_y = chip_of((here + d) % NSETS)
        coefs = tab[4 * set_x + set_y]
        order, log_const = coefs[:, 0:1], coefs[:, 64:65]
        sectorial = math.sqrt(2.0) * jnp.exp(log_const + order * rows[0:1, :])
        cosine = jnp.broadcast_to(rows[1:2, :], (8, SEG))
        turn = order * rows[2:3, :] - 0.25 * parity
        turn = turn - jnp.floor(turn + 0.5)
        square = turn * turn
        harmonic = jnp.full_like(square, COS_TERMS[-1])
        for term in COS_TERMS[-2::-1]:
            harmonic = harmonic * square + term
        lower = sectorial * harmonic
        lowest = jnp.zeros_like(lower)
        keep_level(0, lower)
        for level in range(1, LEV):
            value = (coefs[:, level:level + 1] * cosine) * lower - coefs[:, 64 + level:65 + level] * lowest
            keep_level(level, value)
            lower, lowest = value, lower
            if level % 8 == 7:
                yield
        for slot in range(8):
            for part in range(8):
                dst[slot * LEV:(slot + 1) * LEV, part * 128:(part + 1) * 128] = (
                    dscr[part, slot * PITCH:slot * PITCH + LEV, :].astype(BF16))
            yield

    def whiten(white, src, dst):
        for block in range(SEG // TILE):
            depth = (block + 1) * TILE
            value = lax.dot_general(
                src[:, :depth], white[block * TILE:(block + 1) * TILE, :depth], NT, preferred_element_type=F32)
            dst[:, block * TILE:(block + 1) * TILE] = value.astype(BF16)

    def make_whitened(rows, white):
        pieces = split_rows(rows[3:4, :])

        def put(block, value):
            row = jnp.sum(value, axis=0, keepdims=True)
            wv[:, block * TILE:(block + 1) * TILE] = split_rows(row)

        triangular(pieces, white, put)

    def rhs_terms(src):
        terms = lax.dot_general(wv[...], src[...], NT, preferred_element_type=F32)
        return jnp.broadcast_to(jnp.sum(terms, axis=0, keepdims=True), (8, SET))

    order_z = [z, 3 - z, 3 - z_odd, z_odd]

    def keep_left(src, column):
        for half, kk in enumerate((1 - k, k)):
            for n, zz in enumerate(order_z):
                left[half * 256 + n * 64:half * 256 + n * 64 + 64, column:column + SEG] = (
                    src[pl.ds(pl.multiple_of((2 * zz + kk) * 64, 64), 64), :])

    def product(n, column, src):
        return lax.dot_general(left[:, column:column + SEG], src[n * 256:(n + 1) * 256, :], NT, preferred_element_type=F32)

    def own_terms(d):
        for n in range(2):
            part[d, :, n * 256:(n + 1) * 256] = product(n, 0, filt)
            yield

    interleave(design(rows_l, 0, dbf))
    load.wait()
    make_whitened(rows_l, white_l)

    def own_stage(d, carry):
        whiten(white_l, dbf, filt)

        @pl.when(d == 0)
        def _():
            keep_left(filt, 0)
            sR[0] = rhs_terms(filt)

        @pl.when(d == 0)
        def _():
            for j in range(1, 8):
                table_copy(j).wait()

        interleave(own_terms(d), design(rows_l, d + 1, dbf))
        return carry

    lax.fori_loop(0, NEAR - 1, own_stage, 0)
    whiten(white_l, dbf, filt)
    row_copy.wait()
    interleave(own_terms(NEAR - 1), in_turn(design(rows_o, 0, dbf0), design(rows_o, set_of(0), dbf)))
    for w in whites:
        w.wait()
    whiten(white_o, dbf0, filt0)
    make_whitened(rows_o, white_o)
    keep_left(filt0, SEG)

    def rhs_copy(n):
        return copy(sR.at[n], rR.at[n], r_s.at[n], r_r.at[n], (sibling, z_first, z_second, y_pair)[n])

    def rhs_step(n):
        rhs_copy(n).wait()
        if n < 3:
            sR[n + 1] = sR[n] + rR[n]
            rhs_copy(n + 1).start()
        else:
            for zz in range(4):
                lanes = slice(zz * 128, (zz + 1) * 128)
                rhs_ref[0:1, pl.ds(pl.multiple_of(zz * 256 + y_lo * 128, 128), 128)] = sR[3, 0:1, lanes]
                rhs_ref[0:1, pl.ds(pl.multiple_of(zz * 256 + (1 - y_lo) * 128, 128), 128)] = rR[3, 0:1, lanes]

    def base_of(q):
        set_x, set_y = chip_of(q)
        return (2 * set_x + set_y // 2) * 1024 + (set_y % 2) * 128

    def k_copy(j):
        return copy(sK.at[j], rK.at[j], k_s.at[j], k_r.at[j], sibling)

    def z_copies(j):
        return [copy(sZ.at[j, h], rZ.at[j, h], z_s.at[j, h], z_r.at[j, h], (z_first, z_second)[h]) for h in range(2)]

    def y_copies(j):
        return [copy(sY.at[j, h], rY.at[j, h], y_s.at[j, h], y_r.at[j, h], (z_second, z_first)[h]) for h in range(2)]

    def t_copy(j, slot):
        q = (here + set_of(j)) % NSETS
        return copy(sT.at[j, slot], rT.at[j, 2 * z + k], t_s.at[j, slot], t_r.at[j],
                    at(*chip_of(q), slot // 2, slot % 2))

    def emit(total, d):
        base = base_of((here + d) % NSETS)
        for zz in range(4):
            out_ref[:, pl.ds(pl.multiple_of(base + zz * 256, 128), 128)] = total[:, zz * 128:(zz + 1) * 128]

    def mirror(j, total):
        turned = total.T
        for slot in range(8):
            sT[j, slot] = jnp.concatenate(
                [turned[slot * 64:slot * 64 + 32], turned[slot * 64 + 32:slot * 64 + 64]], axis=1).astype(BF16)

        def send(slot, carry):
            t_copy(j, slot).start()
            return carry

        lax.fori_loop(0, 8, send, 0)

    def finish(j):
        for move in y_copies(j):
            move.wait_recv()
        total = (tot[j % 4] + jnp.concatenate([rY[j, 0], rY[j, 1]], axis=1).astype(F32))
        if not isinstance(j, int) or j < MIRROR:
            mirror(j, total)
        emit(total, 0 if isinstance(j, int) and j == 8 else set_of(j))

    def second(j):
        par = j % 4
        for move in z_copies(j):
            move.wait_recv()
        sY[j, 0] = (keepA[par, 64:128, :] + rZ[j, 0, 0:64, :].astype(F32)).astype(BF16)
        sY[j, 1] = (keepB[par, 64:128, :] + rZ[j, 1, 64:128, :].astype(F32)).astype(BF16)
        for move in y_copies(j):
            move.start()
        tot[par, :, 0:256] = keepA[par, 0:64, :] + rZ[j, 0, 64:128, :].astype(F32)
        tot[par, :, 256:512] = keepB[par, 0:64, :] + rZ[j, 1, 0:64, :].astype(F32)

    def third(j):
        par, now = j % 4, j % 2
        k_copy(j).wait_recv()
        sZ[j, 0] = (own[now, 128:256, 0:256] + rK[j, 128:256, 0:256].astype(F32)).astype(BF16)
        sZ[j, 1] = (own[now, 64:192, 256:512] + rK[j, 64:192, 256:512].astype(F32)).astype(BF16)
        for move in z_copies(j):
            move.start()
        keepA[par] = own[now, 0:128, 0:256] + rK[j, 0:128, 0:256].astype(F32)
        keepB[par, 0:64, :] = own[now, 0:64, 256:512] + rK[j, 0:64, 256:512].astype(F32)
        keepB[par, 64:128, :] = own[now, 192:256, 256:512] + rK[j, 192:256, 256:512].astype(F32)

    def gram(j, d, src):
        for n in range(2):
            lanes = slice(n * 256, (n + 1) * 256)
            total = part[d, :, lanes] + product(n, SEG, src)
            sK[j, :, lanes] = total[0:256].astype(BF16)
            own[j % 2, :, lanes] = total[256:512]
            yield

    def mirrored(j, carry):
        copy(sT.at[j], rT.at[j], t_s.at[j, 0], t_r.at[j], sibling).wait_recv()
        base = base_of((here + NSETS - set_of(j)) % NSETS)
        for zz in range(4):
            for half in range(2):
                lanes = slice(half * 64, half * 64 + 64)
                piece = jnp.concatenate(
                    [rT[j, 2 * zz, :, lanes].astype(F32), rT[j, 2 * zz + 1, :, lanes].astype(F32)], axis=1)
                out_ref[half * 32:half * 32 + 32, pl.ds(pl.multiple_of(base + zz * 256, 128), 128)] = piece

        def sent(slot, inner):
            t_copy(j, slot).wait_send()
            return inner

        lax.fori_loop(0, 8, sent, 0)
        return carry

    sR[0] = sR[0] + rhs_terms(filt0)
    rhs_copy(0).start()

    def stage(i, carry):
        @pl.when(i >= 2)
        def _():
            third(i - 2)

        for n in range(4):
            @pl.when(i == 2 * n + 1)
            def _(n=n):
                rhs_step(n)

        @pl.when(i >= 7)
        def _():
            finish(i - 7)

        whiten(white_o, dbf, filt)

        @pl.when(i >= 4)
        def _():
            second(i - 4)

        interleave(gram(i, set_of(i), filt), design(rows_o, set_of(jnp.minimum(i + 1, 7)), dbf))
        k_copy(i).start()
        return carry

    lax.fori_loop(0, 8, stage, 0)
    third(6)
    finish(1)
    interleave(gram(8, 0, filt0))
    k_copy(8).start()
    second(4)
    third(7)
    finish(2)
    third(8)
    second(5)
    finish(3)
    second(6)
    finish(4)
    second(7)
    finish(5)
    lax.fori_loop(0, 1, mirrored, 0)
    second(8)
    finish(6)
    lax.fori_loop(1, 3, mirrored, 0)
    finish(7)
    lax.fori_loop(3, 4, mirrored, 0)
    finish(8)
    lax.fori_loop(4, MIRROR, mirrored, 0)

    def drain(j, carry):
        k_copy(j).wait_send()
        return carry

    lax.fori_loop(0, NEAR, drain, 0)

    def drain_z(j, carry):
        for move in z_copies(j) + y_copies(j):
            move.wait_send()
        return carry

    lax.fori_loop(0, NEAR, drain_z, 0)


def on_device(sample_index, colatitude, longitude, orders, observed, whitening):
    vmem = pl.BlockSpec(memory_space=pltpu.VMEM)
    V = pltpu.VMEM
    dma = pltpu.SemaphoreType.DMA
    normal, rhs = pl.pallas_call(
        main_kernel,
        out_shape=(jax.ShapeDtypeStruct((64, 8192), F32), jax.ShapeDtypeStruct((1, SEG), F32)),
        in_specs=[vmem] * 5 + [pl.BlockSpec(memory_space=pl.ANY)],
        out_specs=(vmem, vmem),
        scratch_shapes=[
            V((NSETS, 8, 128), F32), V((8, SEG), F32), V((8, SEG), F32),
            V((SEG, SEG), BF16), V((SEG, SEG), BF16),
            V((8, 8 * PITCH, 128), F32), V((SET, SEG), BF16), V((SET, SEG), BF16), V((SET, SEG), BF16), V((SET, SEG), BF16),
            V((NEAR, SET, SET), F32),
            V((SET, 2 * SEG), BF16), V((16, SEG), BF16), V((2, 256, SET), F32),
            V((NEAR, 256, SET), BF16), V((NEAR, 256, SET), BF16),
            V((NEAR, 2, 128, 256), BF16), V((NEAR, 2, 128, 256), BF16),
            V((NEAR, 2, 64, 256), BF16), V((NEAR, 2, 64, 256), BF16),
            V((4, 128, 256), F32), V((4, 128, 256), F32), V((4, 64, SET), F32),
            V((MIRROR, 8, 32, 128), BF16), V((MIRROR, 8, 32, 128), BF16),
            V((4, 8, SET), F32), V((4, 8, SET), F32),
            dma, dma((7,)), dma((7,)), dma, dma, dma((8,)), dma((8,)),
            dma((NEAR,)), dma((NEAR,)), dma((NEAR, 2)), dma((NEAR, 2)),
            dma((NEAR, 2)), dma((NEAR, 2)), dma((MIRROR, 8)), dma((MIRROR,)),
            dma((4,)), dma((4,)),
        ],
        compiler_params=pltpu.CompilerParams(
            collective_id=0, has_side_effects=True, vmem_limit_bytes=60 * 2**20,
        ),
    )(
        sample_index.reshape(1, SEG), colatitude.reshape(128, 128), longitude.reshape(128, 128),
        orders.reshape(1, 16), observed.reshape(1, SEG), whitening,
    )
    rows = 16.0 * SEG
    return normal * (1.0 / rows), rhs.reshape(SEG) * (1.0 / math.sqrt(rows))


def solution(mesh):
    placed = (P("obs"), P(), P(), P("coef"), P("obs"), P("obs", None))
    return jax.shard_map(
        on_device,
        mesh=mesh,
        in_specs=placed,
        out_specs=(P(("coef", "obs"), None), P("coef")),
        check_vma=False,
    )
```

```python
import functools
import math

import jax
import jax.numpy as jnp
from jax import lax
from jax.experimental import pallas as pl
from jax.experimental.pallas import tpu as pltpu
from jax.sharding import PartitionSpec as P

LEV = 64
NMAX = 300
SEG = 1024
SET = 512
NSETS = 16
NEAR = 9
MIRROR = 7
TILE = 256
PITCH = 65
F32 = jnp.float32
BF16 = jnp.bfloat16
MESH = pl.DeviceIdType.MESH
NT = (((1,), (1,)), ((), ()))
COS_TERMS = [(-1.0) ** i * (2.0 * math.pi) ** (2 * i) / math.factorial(2 * i) for i in range(11)]


def prepare(index_ref, colat_ref, long_ref, observed_ref, rows_ref):
    index = index_ref[...]
    high, low = index // 128, index % 128
    pos = lax.broadcasted_iota(jnp.int32, (128, SEG), 0)
    pick_high = (pos == high).astype(F32)
    pick_low = (pos == low).astype(F32)

    def look_up(table):
        found = lax.dot_general(
            table, pick_high, (((0,), (0,)), ((), ())),
            precision=lax.Precision.HIGHEST, preferred_element_type=F32,
        )
        return jnp.sum(found * pick_low, axis=0, keepdims=True)

    colat = look_up(colat_ref[...])
    longitude = look_up(long_ref[...])
    rows_ref[...] = jnp.zeros(rows_ref.shape, F32)
    rows_ref[0:1, :] = jnp.log(jnp.sin(colat))
    rows_ref[1:2, :] = jnp.cos(colat)
    rows_ref[2:3, :] = longitude * (0.5 / math.pi)
    rows_ref[3:4, :] = observed_ref[...]


def make_table(orders_ref):
    place = lax.broadcasted_iota(jnp.int32, (16, 16), 0)
    wanted = (place // 2 % 4) * 4 + (place // 8) * 2 + place % 2
    given = lax.broadcasted_iota(jnp.int32, (16, 16), 1)
    order = jnp.sum(jnp.where(given == wanted, orders_ref[...].astype(F32), 0.0), axis=1, keepdims=True)
    counter = (lax.broadcasted_iota(jnp.int32, (16, 384), 1) + 1).astype(F32)
    log_const = jnp.sum(
        jnp.where(counter <= order, 0.5 * jnp.log((2.0 * counter + 1.0) / (2.0 * counter)), 0.0),
        axis=1, keepdims=True,
    )
    lane = lax.broadcasted_iota(jnp.int32, (16, 128), 1)
    step = jnp.maximum(lane % 64, 1).astype(F32)
    degree = order + step
    rise = jnp.sqrt((2.0 * degree - 1.0) * (2.0 * degree + 1.0) / (step * (degree + order)))
    fall = jnp.sqrt(
        (2.0 * degree + 1.0) * (degree + order - 1.0) * (step - 1.0)
        / ((2.0 * degree - 3.0) * (degree + order) * step)
    )
    table = jnp.where(lane < 64, rise, fall)
    table = jnp.where(lane == 0, order, table)
    return jnp.where(lane == 64, log_const, table)


def in_turn(*parts):
    for part in parts:
        yield from part


def chip_of(q):
    high, low = q // 4, q % 4
    return (high + 2 * low) % 4, (high + 3 * low) % 4


def set_of(j):
    return 8 - (j + 1) % 8


def interleave(*parts):
    parts = list(parts)
    while parts:
        for part in list(parts):
            try:
                next(part)
            except StopIteration:
                parts.remove(part)


def split_rows(row):
    high = row.astype(BF16).astype(F32)
    rest = row - high
    middle = rest.astype(BF16).astype(F32)
    low = rest - middle
    place = lax.broadcasted_iota(jnp.int32, (16, row.shape[1]), 0)
    pieces = jnp.where(place == 0, high, jnp.where(place == 1, middle, jnp.where(place == 2, low, 0.0)))
    return pieces.astype(BF16)


def main_kernel(
    index_ref, colat_ref, long_ref, orders_ref, observed_ref, white_ref, out_ref, rhs_ref,
    tab, rows_l, rows_o, white_l, white_o, dscr, dbf, dbf0, filt, filt0, part, left, wv, own,
    sK, rK, sZ, rZ, sY, rY, keepA, keepB, tot, sT, rT, sR, rR,
    load_s, table_s, table_r, rows_s, rows_r, white_s, white_r,
    k_s, k_r, z_s, z_r, y_s, y_r, t_s, t_r, r_s, r_r,
):
    c, o = lax.axis_index("coef"), lax.axis_index("obs")
    x, y_hi = c // 2, c % 2
    z, y_lo, k = o // 4, (o // 2) % 2, o % 2
    y = 2 * y_hi + y_lo
    low = (y - x + 4) % 4
    here = 4 * ((x + 8 - 2 * low) % 4) + low

    def at(xx, yy, zz, kk):
        return {"coef": 2 * xx + yy // 2, "obs": 4 * zz + 2 * (yy % 2) + kk}

    z_odd = z + 1 - 2 * (z % 2)
    sibling = at(x, y, z, 1 - k)
    z_first = at(x, y, z_odd, k)
    z_second = at(x, y, 3 - z, k)
    y_up = at(x, (y + 1) % 4, z, k)
    y_down = at(x, (y + 3) % 4, z, k)
    y_pair = at(x, y + 1 - 2 * y_lo, z, k)
    near = [sibling, z_first, z_second, y_up, y_down]
    near += [{"coef": (c + j) % 8, "obs": o} for j in range(1, 8)]

    def copy(src, dst, send, recv, device):
        return pltpu.make_async_remote_copy(
            src_ref=src, dst_ref=dst, send_sem=send, recv_sem=recv,
            device_id=device, device_id_type=MESH,
        )

    barrier = pltpu.get_barrier_semaphore()
    for device in near:
        pl.semaphore_signal(barrier, inc=1, device_id=device, device_id_type=MESH)
    load = pltpu.make_async_copy(white_ref, white_l, load_s)
    load.start()
    table = make_table(orders_ref)
    tab[2 * c] = table[0:8]
    tab[2 * c + 1] = table[8:16]
    pl.semaphore_wait(barrier, len(near))

    def table_copy(j):
        mine = tab.at[pl.ds(2 * c, 2)]
        return copy(mine, mine, table_s.at[j - 1], table_r.at[j - 1], {"coef": (c + 8 - j) % 8, "obs": o})

    for j in range(1, 8):
        table_copy(j).start()
    whites = []
    for n, (block, way) in enumerate([(7, 0), (5, 1), (6, 0), (4, 1), (2, 0), (3, 1), (1, 1), (0, 1)]):
        area = (pl.ds(block * 128, 128), pl.ds(0, (block + 1) * 128))
        whites.append(copy(white_ref.at[area], white_o.at[area], white_s.at[n], white_r.at[n],
                           y_up if way == 0 else y_down))
    for w in whites:
        w.start()
    prepare(index_ref, colat_ref, long_ref, observed_ref, rows_l)
    row_copy = copy(rows_l, rows_o, rows_s, rows_r, y_up)
    row_copy.start()

    for block in range(4):
        white_o[block * TILE:block * TILE + 128, block * TILE + 128:(block + 1) * TILE] = jnp.zeros((128, 128), BF16)
    parity = (lax.broadcasted_iota(jnp.int32, (8, SEG), 0) % 2).astype(F32)

    def triangular(operand, white, put):
        for block in range(SEG // TILE):
            depth = (block + 1) * TILE
            put(block, lax.dot_general(
                operand[:, :depth], white[pl.ds(block * TILE, TILE), pl.ds(0, depth)], NT,
                preferred_element_type=F32))

    def keep_level(level, value):
        for part in range(8):
            dscr[part, pl.ds(level, 8, stride=PITCH), :] = value[:, part * 128:(part + 1) * 128]

    def design(rows, d, dst):
        set_x, set_y = chip_of((here + d) % NSETS)
        coefs = tab[4 * set_x + set_y]
        order, log_const = coefs[:, 0:1], coefs[:, 64:65]
        sectorial = math.sqrt(2.0) * jnp.exp(log_const + order * rows[0:1, :])
        cosine = jnp.broadcast_to(rows[1:2, :], (8, SEG))
        turn = order * rows[2:3, :] - 0.25 * parity
        turn = turn - jnp.floor(turn + 0.5)
        square = turn * turn
        harmonic = jnp.full_like(square, COS_TERMS[-1])
        for term in COS_TERMS[-2::-1]:
            harmonic = harmonic * square + term
        lower = sectorial * harmonic
        lowest = jnp.zeros_like(lower)
        keep_level(0, lower)
        for level in range(1, LEV):
            value = (coefs[:, level:level + 1] * cosine) * lower - coefs[:, 64 + level:65 + level] * lowest
            keep_level(level, value)
            lower, lowest = value, lower
            if level % 8 == 7:
                yield
        for slot in range(8):
            for part in range(8):
                dst[slot * LEV:(slot + 1) * LEV, part * 128:(part + 1) * 128] = (
                    dscr[part, slot * PITCH:slot * PITCH + LEV, :].astype(BF16))
            yield

    def whiten(white, src, dst):
        for block in range(SEG // TILE):
            depth = (block + 1) * TILE
            value = lax.dot_general(
                src[:, :depth], white[block * TILE:(block + 1) * TILE, :depth], NT, preferred_element_type=F32)
            dst[:, block * TILE:(block + 1) * TILE] = value.astype(BF16)

    def make_whitened(rows, white):
        pieces = split_rows(rows[3:4, :])

        def put(block, value):
            row = jnp.sum(value, axis=0, keepdims=True)
            wv[:, block * TILE:(block + 1) * TILE] = split_rows(row)

        triangular(pieces, white, put)

    def rhs_terms(src):
        terms = lax.dot_general(wv[...], src[...], NT, preferred_element_type=F32)
        return jnp.broadcast_to(jnp.sum(terms, axis=0, keepdims=True), (8, SET))

    order_z = [z, 3 - z, 3 - z_odd, z_odd]

    def keep_left(src, column):
        for half, kk in enumerate((1 - k, k)):
            for n, zz in enumerate(order_z):
                left[half * 256 + n * 64:half * 256 + n * 64 + 64, column:column + SEG] = (
                    src[pl.ds(pl.multiple_of((2 * zz + kk) * 64, 64), 64), :])

    def product(n, column, src):
        return lax.dot_general(left[:, column:column + SEG], src[n * 256:(n + 1) * 256, :], NT, preferred_element_type=F32)

    def own_terms(d):
        for n in range(2):
            part[d, :, n * 256:(n + 1) * 256] = product(n, 0, filt)
            yield

    interleave(design(rows_l, 0, dbf))
    load.wait()
    make_whitened(rows_l, white_l)

    def own_stage(d, carry):
        whiten(white_l, dbf, filt)

        @pl.when(d == 0)
        def _():
            keep_left(filt, 0)
            sR[0] = rhs_terms(filt)

        @pl.when(d == 0)
        def _():
            for j in range(1, 8):
                table_copy(j).wait()

        interleave(own_terms(d), design(rows_l, d + 1, dbf))
        return carry

    lax.fori_loop(0, NEAR - 1, own_stage, 0)
    whiten(white_l, dbf, filt)
    row_copy.wait()
    interleave(own_terms(NEAR - 1), in_turn(design(rows_o, 0, dbf0), design(rows_o, set_of(0), dbf)))
    for w in whites:
        w.wait()
    whiten(white_o, dbf0, filt0)
    make_whitened(rows_o, white_o)
    keep_left(filt0, SEG)

    def rhs_copy(n):
        return copy(sR.at[n], rR.at[n], r_s.at[n], r_r.at[n], (sibling, z_first, z_second, y_pair)[n])

    def rhs_step(n):
        rhs_copy(n).wait()
        if n < 3:
            sR[n + 1] = sR[n] + rR[n]
            rhs_copy(n + 1).start()
        else:
            for zz in range(4):
                lanes = slice(zz * 128, (zz + 1) * 128)
                rhs_ref[0:1, pl.ds(pl.multiple_of(zz * 256 + y_lo * 128, 128), 128)] = sR[3, 0:1, lanes]
                rhs_ref[0:1, pl.ds(pl.multiple_of(zz * 256 + (1 - y_lo) * 128, 128), 128)] = rR[3, 0:1, lanes]

    def base_of(q):
        set_x, set_y = chip_of(q)
        return (2 * set_x + set_y // 2) * 1024 + (set_y % 2) * 128

    def k_copy(j):
        return copy(sK.at[j], rK.at[j], k_s.at[j], k_r.at[j], sibling)

    def z_copies(j):
        return [copy(sZ.at[j, h], rZ.at[j, h], z_s.at[j, h], z_r.at[j, h], (z_first, z_second)[h]) for h in range(2)]

    def y_copies(j):
        return [copy(sY.at[j, h], rY.at[j, h], y_s.at[j, h], y_r.at[j, h], (z_second, z_first)[h]) for h in range(2)]

    def t_copy(j, slot):
        q = (here + set_of(j)) % NSETS
        return copy(sT.at[j, slot], rT.at[j, 2 * z + k], t_s.at[j, slot], t_r.at[j],
                    at(*chip_of(q), slot // 2, slot % 2))

    def emit(total, d):
        base = base_of((here + d) % NSETS)
        for zz in range(4):
            out_ref[:, pl.ds(pl.multiple_of(base + zz * 256, 128), 128)] = total[:, zz * 128:(zz + 1) * 128]

    def mirror(j, total):
        turned = total.T
        for slot in range(8):
            sT[j, slot] = jnp.concatenate(
                [turned[slot * 64:slot * 64 + 32], turned[slot * 64 + 32:slot * 64 + 64]], axis=1).astype(BF16)

        def send(slot, carry):
            t_copy(j, slot).start()
            return carry

        lax.fori_loop(0, 8, send, 0)

    def finish(j):
        for move in y_copies(j):
            move.wait_recv()
        total = (tot[j % 4] + jnp.concatenate([rY[j, 0], rY[j, 1]], axis=1).astype(F32))
        if not isinstance(j, int) or j < MIRROR:
            mirror(j, total)
        emit(total, 0 if isinstance(j, int) and j == 8 else set_of(j))

    def second(j):
        par = j % 4
        for move in z_copies(j):
            move.wait_recv()
        sY[j, 0] = (keepA[par, 64:128, :] + rZ[j, 0, 0:64, :].astype(F32)).astype(BF16)
        sY[j, 1] = (keepB[par, 64:128, :] + rZ[j, 1, 64:128, :].astype(F32)).astype(BF16)
        for move in y_copies(j):
            move.start()
        tot[par, :, 0:256] = keepA[par, 0:64, :] + rZ[j, 0, 64:128, :].astype(F32)
        tot[par, :, 256:512] = keepB[par, 0:64, :] + rZ[j, 1, 0:64, :].astype(F32)

    def third(j):
        par, now = j % 4, j % 2
        k_copy(j).wait_recv()
        sZ[j, 0] = (own[now, 128:256, 0:256] + rK[j, 128:256, 0:256].astype(F32)).astype(BF16)
        sZ[j, 1] = (own[now, 64:192, 256:512] + rK[j, 64:192, 256:512].astype(F32)).astype(BF16)
        for move in z_copies(j):
            move.start()
        keepA[par] = own[now, 0:128, 0:256] + rK[j, 0:128, 0:256].astype(F32)
        keepB[par, 0:64, :] = own[now, 0:64, 256:512] + rK[j, 0:64, 256:512].astype(F32)
        keepB[par, 64:128, :] = own[now, 192:256, 256:512] + rK[j, 192:256, 256:512].astype(F32)

    def gram(j, d, src):
        for n in range(2):
            lanes = slice(n * 256, (n + 1) * 256)
            total = part[d, :, lanes] + product(n, SEG, src)
            sK[j, :, lanes] = total[0:256].astype(BF16)
            own[j % 2, :, lanes] = total[256:512]
            yield

    def mirrored(j, carry):
        copy(sT.at[j], rT.at[j], t_s.at[j, 0], t_r.at[j], sibling).wait_recv()
        base = base_of((here + NSETS - set_of(j)) % NSETS)
        for zz in range(4):
            for half in range(2):
                lanes = slice(half * 64, half * 64 + 64)
                piece = jnp.concatenate(
                    [rT[j, 2 * zz, :, lanes].astype(F32), rT[j, 2 * zz + 1, :, lanes].astype(F32)], axis=1)
                out_ref[half * 32:half * 32 + 32, pl.ds(pl.multiple_of(base + zz * 256, 128), 128)] = piece

        def sent(slot, inner):
            t_copy(j, slot).wait_send()
            return inner

        lax.fori_loop(0, 8, sent, 0)
        return carry

    sR[0] = sR[0] + rhs_terms(filt0)
    rhs_copy(0).start()

    def stage(i, carry):
        @pl.when(i >= 2)
        def _():
            third(i - 2)

        for n in range(3):
            @pl.when(i == 2 * n + 1)
            def _(n=n):
                rhs_step(n)

        whiten(white_o, dbf, filt)

        @pl.when(i >= 4)
        def _():
            second(i - 4)

        @pl.when(i == 6)
        def _():
            rhs_step(3)

        @pl.when(i >= 6)
        def _():
            finish(i - 6)

        interleave(gram(i, set_of(i), filt), design(rows_o, set_of(jnp.minimum(i + 1, 7)), dbf))
        k_copy(i).start()
        return carry

    lax.fori_loop(0, 8, stage, 0)
    third(6)
    interleave(gram(8, 0, filt0))
    k_copy(8).start()
    third(7)
    second(4)
    finish(2)
    third(8)
    second(5)
    finish(3)
    second(6)
    finish(4)
    second(7)
    finish(5)
    lax.fori_loop(0, 1, mirrored, 0)
    second(8)
    finish(6)
    lax.fori_loop(1, 3, mirrored, 0)
    finish(7)
    lax.fori_loop(3, 4, mirrored, 0)
    finish(8)
    lax.fori_loop(4, MIRROR, mirrored, 0)

    def drain(j, carry):
        k_copy(j).wait_send()
        return carry

    lax.fori_loop(0, NEAR, drain, 0)

    def drain_z(j, carry):
        for move in z_copies(j) + y_copies(j):
            move.wait_send()
        return carry

    lax.fori_loop(0, NEAR, drain_z, 0)


def on_device(sample_index, colatitude, longitude, orders, observed, whitening):
    vmem = pl.BlockSpec(memory_space=pltpu.VMEM)
    V = pltpu.VMEM
    dma = pltpu.SemaphoreType.DMA
    normal, rhs = pl.pallas_call(
        main_kernel,
        out_shape=(jax.ShapeDtypeStruct((64, 8192), F32), jax.ShapeDtypeStruct((1, SEG), F32)),
        in_specs=[vmem] * 5 + [pl.BlockSpec(memory_space=pl.ANY)],
        out_specs=(vmem, vmem),
        scratch_shapes=[
            V((NSETS, 8, 128), F32), V((8, SEG), F32), V((8, SEG), F32),
            V((SEG, SEG), BF16), V((SEG, SEG), BF16),
            V((8, 9 * PITCH + 7, 128), F32), V((SET, SEG), BF16), V((SET, SEG), BF16), V((SET, SEG), BF16), V((SET, SEG), BF16),
            V((NEAR, SET, SET), F32),
            V((SET, 2 * SEG), BF16), V((16, SEG), BF16), V((2, 256, SET), F32),
            V((NEAR, 256, SET), BF16), V((NEAR, 256, SET), BF16),
            V((NEAR, 2, 128, 256), BF16), V((NEAR, 2, 128, 256), BF16),
            V((NEAR, 2, 64, 256), BF16), V((NEAR, 2, 64, 256), BF16),
            V((4, 128, 256), F32), V((4, 128, 256), F32), V((4, 64, SET), F32),
            V((MIRROR, 8, 32, 128), BF16), V((MIRROR, 8, 32, 128), BF16),
            V((4, 8, SET), F32), V((4, 8, SET), F32),
            dma, dma((7,)), dma((7,)), dma, dma, dma((8,)), dma((8,)),
            dma((NEAR,)), dma((NEAR,)), dma((NEAR, 2)), dma((NEAR, 2)),
            dma((NEAR, 2)), dma((NEAR, 2)), dma((MIRROR, 8)), dma((MIRROR,)),
            dma((4,)), dma((4,)),
        ],
        compiler_params=pltpu.CompilerParams(
            collective_id=0, has_side_effects=True, vmem_limit_bytes=60 * 2**20,
        ),
    )(
        sample_index.reshape(1, SEG), colatitude.reshape(128, 128), longitude.reshape(128, 128),
        orders.reshape(1, 16), observed.reshape(1, SEG), whitening,
    )
    rows = 16.0 * SEG
    return normal * (1.0 / rows), rhs.reshape(SEG) * (1.0 / math.sqrt(rows))


def solution(mesh):
    placed = (P("obs"), P(), P(), P("coef"), P("obs"), P("obs", None))
    return jax.shard_map(
        on_device,
        mesh=mesh,
        in_specs=placed,
        out_specs=(P(("coef", "obs"), None), P("coef")),
        check_vma=False,
    )
```
